256 devices in a mesh: fsdp: 16 (over x_hi, y, core), tensor: 16 (over x_lo, z).
Axes of the slice: x: 4 (x_hi: 2, x_lo: 2; x = x_hi * 2 + x_lo), y: 4, z: 8, core: 2. Of those that a mesh axis runs over, the one named last changes fastest.
Arguments:
- tokens: bfloat16 [2048, 4096], P(('fsdp', 'tensor')), may hold values from -19 to 19
- targets: bfloat16 [2048, 4096], P(('fsdp', 'tensor')), may hold values from -6 to 6
- gate_up: bfloat16 [4096, 2, 7168], P(None, None, 'tensor'), may hold values from -0.09375 to 0.09375
- down_weight: bfloat16 [7168, 4096], P('tensor'), may hold values from -0.0625 to 0.0625
- direction: bfloat16 [4096, 2, 7168], P('fsdp', None, 'tensor'), may hold values from -47 to 47
- previous: bfloat16 [4096, 2, 7168], P('fsdp', None, 'tensor'), may hold values from -47 to 47
- beta_prev: float32 [], replicated, may hold values from 0.5 to 2
Outputs:
- new_direction: bfloat16 [4096, 2, 7168], P('fsdp', None, 'tensor')
- tri_diagonal: float32 [], replicated
- tri_offdiagonal: float32 [], replicated
The draws below stay inside these ranges and needn't reach their ends.
All inputs are finite; a program needn't handle non-finite values.
Results may differ from the reference program's by a relative error of at most 0.025.
Values may be sent and summed in bfloat16 or wider, within the bound.
No kernel may reach another device: no remote copies, remote signals or barrier semaphores. Data moves between devices by JAX's collectives and lax.ppermute only.
A program may use at most 64 MiB of HBM per device.

```python
import math
import jax
import jax.numpy as jnp
from jax import lax

D = 4096
FF = 7168
TOK_DEV = 128
TOKENS = 2048
GROUPS = 16


def lanczos_field(key):
    first_key, second_key, third_key = jax.random.split(key, 3)
    base_values = jnp.clip(jax.random.normal(first_key, (D, 2, FF), jnp.float32), -4.0, 4.0)
    row_scale = jnp.exp(jax.random.uniform(second_key, (D, 1, 1), jnp.float32, 0.0, math.log(10.0)))
    row_rise = jnp.exp(math.log(3.0) * jnp.arange(D, dtype=jnp.float32) / D).reshape(D, 1, 1)
    column_scale = jnp.exp(jax.random.uniform(third_key, (1, 1, FF), jnp.float32, 0.0, math.log(10.0)))
    column_rise = jnp.exp(math.log(3.0) * jnp.arange(FF, dtype=jnp.float32) / FF).reshape(1, 1, FF)
    return (base_values * (row_scale * row_rise) * (column_scale * column_rise) / 78.0).astype(jnp.bfloat16)


def draw_tokens(key, part):
    key = jax.random.fold_in(key, 11)
    first_key, second_key = jax.random.split(key, 2)
    base_values = jnp.clip(jax.random.normal(first_key, (TOKENS, D), jnp.float32), -4.0, 4.0)
    feature_scale = jnp.exp(jax.random.uniform(second_key, (D,), jnp.float32, 0.0, math.log(10.0)))
    feature_rise = jnp.exp(math.log(3.0) * jnp.arange(D, dtype=jnp.float32) / D)
    return (base_values * (feature_scale * feature_rise / 9.0)).astype(jnp.bfloat16)


def draw_direction(key, part):
    key = jax.random.fold_in(key, 21)
    return lanczos_field(key)


def draw_previous(key, part):
    key = jax.random.fold_in(key, 37)
    return lanczos_field(key)


def level_of(rng, shape, pieces, least, top_value):
    factor_of, own = 1.0, jax.random.fold_in(rng, 6)
    for axis_at, shards_of in pieces:
        steps = jnp.exp(jax.random.uniform(jax.random.fold_in(own, axis_at), (shards_of,), jnp.float32, least / len(pieces), top_value / len(pieces)))
        factor_of = factor_of * jnp.repeat(steps, shape[axis_at] // shards_of).reshape([-1 if axis == axis_at else 1 for axis in range(len(shape))])
    return factor_of


def gaussian(stream_key, dims, width, bound, pieces=(), kind=jnp.bfloat16):
    entries = jax.random.normal(stream_key, dims, jnp.float32) * width
    if len(pieces) > 0:
        entries = level_of(stream_key, dims, pieces, -0.22, 0.18) * entries
    return jnp.clip(entries, min=-bound, max=bound).astype(kind)


def setup_inputs(seed: int = 0) -> dict:
    streams_of = jax.random.split(jax.random.key(seed), 8)
    return {
        "tokens": draw_tokens(jax.random.fold_in(streams_of[7], 71), 0),
        "targets": gaussian(streams_of[1], (TOKENS, D), 1.0, 6.0, ((0, 256),)),
        "gate_up": gaussian(streams_of[2], (D, 2, FF), D ** -0.5, 0.09375, ((2, 16),)),
        "down_weight": gaussian(streams_of[3], (FF, D), FF ** -0.5, 0.0625, ((0, 16),)),
        "direction": draw_direction(jax.random.fold_in(streams_of[7], 71), 0),
        "previous": draw_previous(jax.random.fold_in(streams_of[7], 71), 0),
        "beta_prev": jnp.clip(jnp.exp(jax.random.uniform(streams_of[6], (), jnp.float32, math.log(0.5), math.log(2.0))), 0.5, 2.0),
    }


def silu_parts(gate_pre):
    sigma_gate = jax.nn.sigmoid(gate_pre)
    silu_value = gate_pre * sigma_gate
    silu_slope = sigma_gate * (1.0 + gate_pre * (1.0 - sigma_gate))
    silu_curve = sigma_gate * (1.0 - sigma_gate) * (2.0 + gate_pre * (1.0 - 2.0 * sigma_gate))
    return (silu_value, silu_slope, silu_curve)

def reference(tokens, targets, gate_up, down_weight, direction, previous, beta_prev):
    projected = jnp.dot(tokens, gate_up.reshape(D, 2 * FF), preferred_element_type=jnp.float32).reshape(TOKENS, 2, FF)
    gate_pre = projected[:, 0]
    up_pre = projected[:, 1]
    silu_value, silu_slope, silu_curve = silu_parts(gate_pre)
    hidden_act = (silu_value * up_pre).astype(jnp.bfloat16)
    tangent = jnp.dot(tokens, direction.reshape(D, 2 * FF), preferred_element_type=jnp.float32).reshape(TOKENS, 2, FF)
    tangent_gate = tangent[:, 0]
    tangent_up = tangent[:, 1]
    tangent_act = (silu_slope * tangent_gate * up_pre + silu_value * tangent_up).astype(jnp.bfloat16)
    output_sum = jnp.dot(hidden_act, down_weight, preferred_element_type=jnp.float32)
    tangent_sum = jnp.dot(tangent_act, down_weight, preferred_element_type=jnp.float32)
    error_rows = ((output_sum - targets.astype(jnp.float32)) / TOKENS).astype(jnp.bfloat16)
    tangent_error = (tangent_sum / TOKENS).astype(jnp.bfloat16)
    back_error = jnp.dot(error_rows, down_weight.T, preferred_element_type=jnp.float32)
    back_tangent = jnp.dot(tangent_error, down_weight.T, preferred_element_type=jnp.float32)
    grad_gate = back_tangent * up_pre * silu_slope + back_error * (tangent_up * silu_slope + up_pre * silu_curve * tangent_gate)
    grad_up = back_tangent * silu_value + back_error * silu_slope * tangent_gate
    tangent_grad = jnp.stack([grad_gate, grad_up], 1).astype(jnp.bfloat16).reshape(TOKENS, 2 * FF)
    group_tokens = tokens.reshape(GROUPS, TOK_DEV, D)
    group_grads = tangent_grad.reshape(GROUPS, TOK_DEV, 2 * FF)

    def add_group(running, group_pair):
        token_block, grad_block = group_pair
        part_sum = lax.dot_general(token_block, grad_block, (((0,), (0,)), ((), ())), preferred_element_type=jnp.float32)
        rounded = lax.optimization_barrier(part_sum.astype(jnp.bfloat16))
        return (running + rounded.astype(jnp.float32), None)
    total_sum, unused = lax.scan(add_group, jnp.zeros((D, 2 * FF), jnp.float32), (group_tokens, group_grads))
    curvature = total_sum.reshape(D, 2, FF)
    current = direction.astype(jnp.float32)
    earlier = previous.astype(jnp.float32)
    tri_diagonal = jnp.mean(curvature * current)
    residual = curvature - tri_diagonal * current - beta_prev * earlier
    tri_offdiagonal = jnp.sqrt(jnp.mean(residual * residual) + 1e-06)
    new_direction = (residual / tri_offdiagonal).astype(jnp.bfloat16)
    return (new_direction, tri_diagonal, tri_offdiagonal)
```

```python
import jax
import jax.numpy as jnp
from jax import lax
from jax.sharding import Mesh, PartitionSpec as P

BF = jnp.bfloat16
F32 = jnp.float32
AXES = ("x_hi", "y", "core", "x_lo", "z")
SIZES = (2, 4, 2, 2, 8)


def swap(value, axis, step=1):
    size = lax.axis_size(axis)
    return lax.ppermute(value, axis, [(i, i ^ step) for i in range(size)])


def silu_parts(gate_pre):
    sigma_gate = jax.nn.sigmoid(gate_pre)
    silu_value = gate_pre * sigma_gate
    silu_slope = sigma_gate * (1.0 + gate_pre * (1.0 - sigma_gate))
    silu_curve = sigma_gate * (1.0 - sigma_gate) * (2.0 + gate_pre * (1.0 - 2.0 * sigma_gate))
    return (silu_value, silu_slope, silu_curve)


def gather_tensor(block):
    along = [block] + [swap(block, "z", d) for d in range(1, 8)]
    groups = [jnp.concatenate(along[0:3], 0), jnp.concatenate(along[3:6], 0), jnp.concatenate(along[6:8], 0)]
    across = [swap(g, "x_lo") for g in groups]
    return groups + across


def scatter_tensor(partial):
    rows, width = partial.shape
    halves = partial.reshape(2, 8, rows // 16, width)
    other = swap(halves[1], "x_lo")
    mine = (halves[0].astype(F32) + other.astype(F32)).astype(BF)
    total = mine[0].astype(F32)
    for d in range(1, 8):
        total = total + swap(mine[d], "z", d).astype(F32)
    return total


def dot(a, b, dims):
    return lax.dot_general(a, b, (dims, ((), ())), preferred_element_type=F32)


def total_over_devices(values):
    k = values.shape[0]
    tile = jnp.broadcast_to(jnp.pad(values, (0, 8 - k))[:, None], (8, 128))
    tile = tile + swap(tile, "core")
    for axes, size in (("z", 8), (("x_hi", "y", "x_lo"), 16)):
        sent = jnp.broadcast_to(tile[None], (size, 8, 128))
        tile = lax.all_to_all(sent, axes, 0, 0, tiled=True).sum(0)
    return tile[:k, 0]


def per_device(tokens, targets, gate_up, down_weight, direction, previous, beta_prev):
    width = tokens.shape[1]
    hidden = down_weight.shape[0]
    own_rows = direction.shape[0]
    token_total = tokens.shape[0] * 256
    gate_up_t = gate_up.transpose(1, 2, 0).reshape(2 * hidden, width)
    current_t = direction.transpose(1, 2, 0).reshape(2 * hidden, own_rows)
    earlier_t = previous.transpose(1, 2, 0).reshape(2 * hidden, own_rows)
    x_hi, y_at, core = (lax.axis_index(n) for n in ("x_hi", "y", "core"))

    current_far = swap(current_t, "x_hi")
    near = lax.all_gather(current_t, "y", axis=1, tiled=True)
    far = lax.all_gather(current_far, "y", axis=1, tiled=True)

    group_rows = jnp.concatenate(gather_tensor(tokens), 0)
    projected = dot(gate_up_t, group_rows, ((1,), (1,)))
    gate_pre, up_pre = projected[:hidden], projected[hidden:]
    silu_value, silu_slope, silu_curve = silu_parts(gate_pre)
    hidden_act = (silu_value * up_pre).astype(BF)
    output_part = dot(hidden_act, down_weight, ((0,), (0,))).astype(BF)
    output_sum = scatter_tensor(output_part)

    columns = group_rows.reshape(-1, 2, 4, 2, own_rows)

    def pick(value, at, dim):
        return lax.dynamic_index_in_dim(value, at, dim, keepdims=False)

    by_x = [pick(columns, x_hi, 1), pick(columns, 1 - x_hi, 1)]
    by_xc = [[pick(part, core, 2), pick(part, 1 - core, 2)] for part in by_x]

    tangent = 0.0
    for at, piece in enumerate((near, far)):
        for side, block in enumerate((piece, swap(piece, "core"))):
            tangent = tangent + dot(block, by_xc[at][side].reshape(-1, 4 * own_rows), ((1,), (1,)))
    tangent_gate, tangent_up = tangent[:hidden], tangent[hidden:]
    tangent_act = (silu_slope * tangent_gate * up_pre + silu_value * tangent_up).astype(BF)
    tangent_part = dot(tangent_act, down_weight, ((0,), (0,))).astype(BF)
    tangent_sum = scatter_tensor(tangent_part)

    error_rows = ((output_sum - targets.astype(F32)) / token_total).astype(BF)
    tangent_error = (tangent_sum / token_total).astype(BF)
    errors = jnp.concatenate(
        [p.reshape(-1, 2, 8, width) for p in gather_tensor(jnp.concatenate([error_rows, tangent_error], 0))], 0
    )
    back_error = dot(down_weight, errors[:, 0].reshape(-1, width), ((1,), (1,)))
    back_tangent = dot(down_weight, errors[:, 1].reshape(-1, width), ((1,), (1,)))

    kept = [columns_x for columns_x in (by_x[0], swap(by_x[1], "x_hi"))]
    own_columns = []
    for part in kept:
        same = pick(part, core, 2)
        cross = swap(pick(part, 1 - core, 2), "core")
        own_columns.append([same, cross])
    own_columns = jnp.stack([jnp.stack(pair) for pair in own_columns])
    by_y = [pick(own_columns, y_at, 3)]
    for d in range(1, 4):
        by_y.append(swap(pick(own_columns, y_at ^ d, 3), "y", d))
    by_y = jnp.stack(by_y)
    ordered = jnp.stack([pick(by_y, y_at ^ at, 0) for at in range(4)], 2)

    grad_gate = back_tangent * up_pre * silu_slope + back_error * (
        tangent_up * silu_slope + up_pre * silu_curve * tangent_gate
    )
    grad_up = back_tangent * silu_value + back_error * silu_slope * tangent_gate
    tangent_grad = jnp.concatenate([grad_gate, grad_up], 0).astype(BF)
    grad_far = swap(tangent_grad, "x_hi")
    curvature = 0.0
    for at, piece in enumerate((tangent_grad, grad_far)):
        piece = lax.all_gather(piece, "y", axis=1, tiled=True)
        for side, block in enumerate((piece, swap(piece, "core"))):
            curvature = curvature + dot(block, ordered[at, side].reshape(-1, own_rows), ((1,), (0,)))

    current = current_t.astype(F32)
    shifted = curvature - beta_prev * earlier_t.astype(F32)
    sums = total_over_devices(
        jnp.stack(
            [
                jnp.sum(curvature * current),
                jnp.sum(shifted * shifted),
                jnp.sum(shifted * current),
                jnp.sum(current * current),
            ]
        )
    )
    entry_count = 2 * own_rows * hidden * 256
    rayleigh = sums[0] / entry_count
    square = (sums[1] - 2.0 * rayleigh * sums[2] + rayleigh * rayleigh * sums[3]) / entry_count
    offdiagonal = jnp.sqrt(jnp.maximum(square, 0.0) + 1e-06)
    new_direction = ((shifted - rayleigh * current) / offdiagonal).astype(BF)
    new_direction = new_direction.reshape(2, hidden, own_rows).transpose(2, 0, 1)
    return (new_direction, rayleigh, offdiagonal)


def solution(mesh):
    fine = Mesh(mesh.devices.reshape(SIZES), AXES)
    fsdp, tensor = AXES[:3], AXES[3:]
    placed = (
        P(fsdp + tensor, None),
        P(fsdp + tensor, None),
        P(None, None, tensor),
        P(tensor, None),
        P(fsdp, None, tensor),
        P(fsdp, None, tensor),
        P(),
    )
    return jax.shard_map(
        per_device,
        mesh=fine,
        in_specs=placed,
        out_specs=(P(fsdp, None, tensor), P(), P()),
        check_vma=False,
    )
```

```python
import jax
import jax.numpy as jnp
from jax import lax
from jax.sharding import Mesh, PartitionSpec as P

BF = jnp.bfloat16
F32 = jnp.float32
AXES = ("x_hi", "y", "core", "x_lo", "z")
SIZES = (2, 4, 2, 2, 8)


def swap(value, axis, step=1):
    size = lax.axis_size(axis)
    return lax.ppermute(value, axis, [(i, i ^ step) for i in range(size)])


def silu_parts(gate_pre):
    sigma_gate = jax.nn.sigmoid(gate_pre)
    silu_value = gate_pre * sigma_gate
    silu_slope = sigma_gate * (1.0 + gate_pre * (1.0 - sigma_gate))
    silu_curve = sigma_gate * (1.0 - sigma_gate) * (2.0 + gate_pre * (1.0 - 2.0 * sigma_gate))
    return (silu_value, silu_slope, silu_curve)


def gather_tensor(block):
    along = [block] + [swap(block, "z", d) for d in range(1, 8)]
    groups = [jnp.concatenate(along[0:3], 0), jnp.concatenate(along[3:6], 0), jnp.concatenate(along[6:8], 0)]
    across = [swap(g, "x_lo") for g in groups]
    return groups + across


def fold_x(partial):
    rows, width = partial.shape
    halves = partial.reshape(2, 8, rows // 16, width)
    other = swap(halves[1], "x_lo")
    return (halves[0].astype(F32) + other.astype(F32)).astype(BF)


def fold_z(folded):
    total = folded[0].astype(F32)
    for d in range(1, 8):
        total = total + swap(folded[d], "z", d).astype(F32)
    return total


def dot(a, b, dims):
    return lax.dot_general(a, b, (dims, ((), ())), preferred_element_type=F32)


def total_over_devices(values):
    k = values.shape[0]
    tile = jnp.broadcast_to(jnp.pad(values, (0, 8 - k))[:, None], (8, 128))
    tile = tile + swap(tile, "core")
    for axes, size in (("z", 8), (("x_hi", "y", "x_lo"), 16)):
        sent = jnp.broadcast_to(tile[None], (size, 8, 128))
        tile = lax.all_to_all(sent, axes, 0, 0, tiled=True).sum(0)
    return tile[:k, 0]


def per_device(tokens, targets, gate_up, down_weight, direction, previous, beta_prev):
    width = tokens.shape[1]
    hidden = down_weight.shape[0]
    own_rows = direction.shape[0]
    token_total = tokens.shape[0] * 256
    gate_up_t = gate_up.transpose(1, 2, 0).reshape(2 * hidden, width)
    current_t = direction.transpose(1, 2, 0).reshape(2 * hidden, own_rows)
    earlier_t = previous.transpose(1, 2, 0).reshape(2 * hidden, own_rows)
    x_hi, y_at, core = (lax.axis_index(n) for n in ("x_hi", "y", "core"))

    near = lax.all_gather(current_t, "y", axis=1, tiled=True)
    current_far = swap(current_t, "x_hi")

    group_rows = jnp.concatenate(gather_tensor(tokens), 0)
    group_rows, current_far = lax.optimization_barrier((group_rows, current_far))
    far = [current_far] + [swap(current_far, "y", d) for d in range(1, 4)]

    projected = dot(gate_up_t, group_rows, ((1,), (1,)))
    gate_pre, up_pre = projected[:hidden], projected[hidden:]
    silu_value, silu_slope, silu_curve = silu_parts(gate_pre)
    hidden_act = (silu_value * up_pre).astype(BF)
    output_part = dot(hidden_act, down_weight, ((0,), (0,))).astype(BF)
    output_fold = fold_x(output_part)

    def owners_of(which):
        return jnp.concatenate(
            [
                lax.dynamic_slice_in_dim(group_rows, (at * 2 + which) * own_rows, own_rows, 1)
                for at in range(8)
            ],
            1,
        )

    def cut(value, start, size):
        return lax.dynamic_slice_in_dim(value, start * own_rows, size * own_rows, value.ndim - 1)

    by_core = [owners_of(core), owners_of(1 - core)]

    both = jnp.stack([by_core[0], swap(by_core[1], "core")])
    both = jnp.stack([cut(both, x_hi * 4, 4), swap(cut(both, 4 - x_hi * 4, 4), "x_hi")])
    by_y = jnp.stack(
        [cut(both, y_at, 1)] + [swap(cut(both, y_at ^ d, 1), "y", d) for d in range(1, 4)]
    )

    def group_y(at):
        return lax.dynamic_index_in_dim(by_y, y_at ^ at, 0, keepdims=False)

    ordered = jnp.stack([group_y(at) for at in range(4)], 2)

    tangent = 0.0
    for side, block in enumerate((near, swap(near, "core"))):
        tangent = tangent + dot(block, cut(by_core[side], x_hi * 4, 4), ((1,), (1,)))
    for d in range(4):
        for side, block in enumerate((far[d], swap(far[d], "core"))):
            tangent = tangent + dot(block, cut(by_core[side], (1 - x_hi) * 4 + (y_at ^ d), 1), ((1,), (1,)))
    tangent_gate, tangent_up = tangent[:hidden], tangent[hidden:]
    tangent_act = (silu_slope * tangent_gate * up_pre + silu_value * tangent_up).astype(BF)
    tangent_part = dot(tangent_act, down_weight, ((0,), (0,))).astype(BF)
    tangent_fold = fold_x(tangent_part)
    sums = fold_z(jnp.concatenate([output_fold, tangent_fold], 1))
    rows = targets.shape[0]
    error_rows = ((sums[:rows] - targets.astype(F32)) / token_total).astype(BF)
    tangent_error = (sums[rows:] / token_total).astype(BF)
    errors = jnp.concatenate(
        [p.reshape(-1, 2, 8, width) for p in gather_tensor(jnp.concatenate([error_rows, tangent_error], 0))], 0
    )
    back_error = dot(down_weight, errors[:, 0].reshape(-1, width), ((1,), (1,)))
    back_tangent = dot(down_weight, errors[:, 1].reshape(-1, width), ((1,), (1,)))

    grad_gate = back_tangent * up_pre * silu_slope + back_error * (
        tangent_up * silu_slope + up_pre * silu_curve * tangent_gate
    )
    grad_up = back_tangent * silu_value + back_error * silu_slope * tangent_gate
    tangent_grad = jnp.concatenate([grad_gate, grad_up], 0).astype(BF)
    grad_far = swap(tangent_grad, "x_hi")
    curvature = 0.0
    for at, piece in enumerate((tangent_grad, grad_far)):
        piece = lax.all_gather(piece, "y", axis=1, tiled=True)
        for side, block in enumerate((piece, swap(piece, "core"))):
            curvature = curvature + dot(block, ordered[at, side].reshape(-1, own_rows), ((1,), (0,)))

    current = current_t.astype(F32)
    shifted = curvature - beta_prev * earlier_t.astype(F32)
    sums = total_over_devices(
        jnp.stack(
            [
                jnp.sum(curvature * current),
                jnp.sum(shifted * shifted),
                jnp.sum(shifted * current),
                jnp.sum(current * current),
            ]
        )
    )
    entry_count = 2 * own_rows * hidden * 256
    rayleigh = sums[0] / entry_count
    square = (sums[1] - 2.0 * rayleigh * sums[2] + rayleigh * rayleigh * sums[3]) / entry_count
    offdiagonal = jnp.sqrt(jnp.maximum(square, 0.0) + 1e-06)
    new_direction = ((shifted - rayleigh * current) / offdiagonal).astype(BF)
    new_direction = new_direction.reshape(2, hidden, own_rows).transpose(2, 0, 1)
    return (new_direction, rayleigh, offdiagonal)


def solution(mesh):
    fine = Mesh(mesh.devices.reshape(SIZES), AXES)
    fsdp, tensor = AXES[:3], AXES[3:]
    placed = (
        P(fsdp + tensor, None),
        P(fsdp + tensor, None),
        P(None, None, tensor),
        P(tensor, None),
        P(fsdp, None, tensor),
        P(fsdp, None, tensor),
        P(),
    )
    return jax.shard_map(
        per_device,
        mesh=fine,
        in_specs=placed,
        out_specs=(P(fsdp, None, tensor), P(), P()),
        check_vma=False,
    )
```

```python
import jax
import jax.numpy as jnp
from jax import lax
from jax.sharding import Mesh, PartitionSpec as P

BF = jnp.bfloat16
F32 = jnp.float32
AXES = ("x_hi", "y", "core", "x_lo", "z")
SIZES = (2, 4, 2, 2, 8)


def swap(value, axis, step=1):
    size = lax.axis_size(axis)
    return lax.ppermute(value, axis, [(i, i ^ step) for i in range(size)])


def silu_parts(gate_pre):
    sigma_gate = jax.nn.sigmoid(gate_pre)
    silu_value = gate_pre * sigma_gate
    silu_slope = sigma_gate * (1.0 + gate_pre * (1.0 - sigma_gate))
    silu_curve = sigma_gate * (1.0 - sigma_gate) * (2.0 + gate_pre * (1.0 - 2.0 * sigma_gate))
    return (silu_value, silu_slope, silu_curve)


def neighbour(value):
    return lax.ppermute(value, "z", [(i, (i + 1) % 8 if i % 2 else (i - 1) % 8) for i in range(8)])


def by_pair(value):
    at = lax.axis_index("z") % 4
    return jnp.where((at == 1) | (at == 2), value[jnp.array([1, 0, 3, 2])], value[::-1])


def gather_z(block):
    half = block.shape[1] // 2
    even = jnp.stack([block] + [swap(block, "z", d) for d in (2, 4, 6)])
    odd = jnp.concatenate([swap(even[..., :half], "z"), by_pair(neighbour(even[..., half:]))], 2)
    return even, odd


def gather_x(even, odd):
    return jnp.concatenate([even, odd, swap(even, "x_lo"), swap(odd, "x_lo")], 0)


def fold_x(partial):
    rows, width = partial.shape
    halves = partial.reshape(2, 2, 4, rows // 16, width)
    other = swap(halves[1], "x_lo")
    return (halves[0].astype(F32) + other.astype(F32)).astype(BF)


def fold_z(folded):
    half = folded.shape[-1] // 2
    even, odd = folded[0], folded[1]
    other = jnp.concatenate([swap(odd[..., :half], "z"), by_pair(neighbour(odd[..., half:]))], 2)
    even = (even.astype(F32) + other.astype(F32)).astype(BF)
    total = even[0].astype(F32)
    for at in range(1, 4):
        total = total + swap(even[at], "z", 2 * at).astype(F32)
    return total


def dot(a, b, dims):
    return lax.dot_general(a, b, (dims, ((), ())), preferred_element_type=F32)


def total_over_devices(values):
    k = values.shape[0]
    tile = jnp.broadcast_to(jnp.pad(values, (0, 8 - k))[:, None], (8, 128))
    tile = tile + swap(tile, "core")
    for axes, size in (("z", 8), (("x_hi", "y", "x_lo"), 16)):
        sent = jnp.broadcast_to(tile[None], (size, 8, 128))
        tile = lax.all_to_all(sent, axes, 0, 0, tiled=True).sum(0)
    return tile[:k, 0]


def per_device(tokens, targets, gate_up, down_weight, direction, previous, beta_prev):
    width = tokens.shape[1]
    hidden = down_weight.shape[0]
    own_rows = direction.shape[0]
    token_total = tokens.shape[0] * 256
    gate_up_t = gate_up.transpose(1, 2, 0).reshape(2 * hidden, width)
    current_t = direction.transpose(1, 2, 0).reshape(2 * hidden, own_rows)
    earlier_t = previous.transpose(1, 2, 0).reshape(2 * hidden, own_rows)
    x_hi, y_at, core = (lax.axis_index(n) for n in ("x_hi", "y", "core"))

    near = lax.all_gather(current_t, "y", axis=1, tiled=True)
    current_far = swap(current_t, "x_hi")

    even, odd = gather_z(tokens)
    even, odd, current_far = lax.optimization_barrier((even, odd, current_far))
    group_rows = gather_x(even, odd).reshape(-1, width)
    far = [current_far] + [swap(current_far, "y", d) for d in range(1, 4)]

    projected = dot(gate_up_t, group_rows, ((1,), (1,)))
    gate_pre, up_pre = projected[:hidden], projected[hidden:]
    silu_value, silu_slope, silu_curve = silu_parts(gate_pre)
    hidden_act = (silu_value * up_pre).astype(BF)
    output_part = dot(hidden_act, down_weight, ((0,), (0,))).astype(BF)
    output_fold = fold_x(output_part)

    def owners_of(which):
        return jnp.concatenate(
            [
                lax.dynamic_slice_in_dim(group_rows, (at * 2 + which) * own_rows, own_rows, 1)
                for at in range(8)
            ],
            1,
        )

    def cut(value, start, size):
        return lax.dynamic_slice_in_dim(value, start * own_rows, size * own_rows, value.ndim - 1)

    by_core = [owners_of(core), owners_of(1 - core)]

    both = jnp.stack([by_core[0], swap(by_core[1], "core")])
    both = jnp.stack([cut(both, x_hi * 4, 4), swap(cut(both, 4 - x_hi * 4, 4), "x_hi")])
    tangent = 0.0
    for side, block in enumerate((near, swap(near, "core"))):
        tangent = tangent + dot(block, cut(by_core[side], x_hi * 4, 4), ((1,), (1,)))
    for d in range(4):
        for side, block in enumerate((far[d], swap(far[d], "core"))):
            tangent = tangent + dot(block, cut(by_core[side], (1 - x_hi) * 4 + (y_at ^ d), 1), ((1,), (1,)))
    tangent_gate, tangent_up = tangent[:hidden], tangent[hidden:]
    tangent_act = (silu_slope * tangent_gate * up_pre + silu_value * tangent_up).astype(BF)
    tangent_part = dot(tangent_act, down_weight, ((0,), (0,))).astype(BF)
    tangent_fold = fold_x(tangent_part)
    output_sum = fold_z(output_fold)
    tangent_sum = fold_z(tangent_fold)
    error_rows = ((output_sum - targets.astype(F32)) / token_total).astype(BF)
    tangent_error = (tangent_sum / token_total).astype(BF)
    errors = jnp.concatenate([error_rows, tangent_error], 0)
    errors, both = lax.optimization_barrier((errors, both))
    errors = gather_x(*gather_z(errors)).reshape(16, 2, -1, width)
    own_columns = jnp.stack(
        [cut(both, y_at, 1)] + [swap(cut(both, y_at ^ d, 1), "y", d) for d in range(1, 4)], 2
    )
    back_error = dot(down_weight, errors[:, 0].reshape(-1, width), ((1,), (1,)))
    back_tangent = dot(down_weight, errors[:, 1].reshape(-1, width), ((1,), (1,)))

    grad_gate = back_tangent * up_pre * silu_slope + back_error * (
        tangent_up * silu_slope + up_pre * silu_curve * tangent_gate
    )
    grad_up = back_tangent * silu_value + back_error * silu_slope * tangent_gate
    tangent_grad = jnp.concatenate([grad_gate, grad_up], 0).astype(BF)
    along = [tangent_grad] + [swap(tangent_grad, "y", d) for d in range(1, 4)]
    cross = swap(tangent_grad, "x_hi")
    cross = [cross, swap(cross, "y", 1), swap(along[2], "x_hi"), swap(cross, "y", 3)]
    curvature = 0.0
    for at, pieces in enumerate((along, cross)):
        piece = jnp.concatenate(pieces, 1)
        for side, block in enumerate((piece, swap(piece, "core"))):
            curvature = curvature + dot(block, own_columns[at, side].reshape(-1, own_rows), ((1,), (0,)))

    current = current_t.astype(F32)
    shifted = curvature - beta_prev * earlier_t.astype(F32)
    sums = total_over_devices(
        jnp.stack(
            [
                jnp.sum(curvature * current),
                jnp.sum(shifted * shifted),
                jnp.sum(shifted * current),
                jnp.sum(current * current),
            ]
        )
    )
    entry_count = 2 * own_rows * hidden * 256
    rayleigh = sums[0] / entry_count
    square = (sums[1] - 2.0 * rayleigh * sums[2] + rayleigh * rayleigh * sums[3]) / entry_count
    offdiagonal = jnp.sqrt(jnp.maximum(square, 0.0) + 1e-06)
    new_direction = ((shifted - rayleigh * current) / offdiagonal).astype(BF)
    new_direction = new_direction.reshape(2, hidden, own_rows).transpose(2, 0, 1)
    return (new_direction, rayleigh, offdiagonal)


def solution(mesh):
    fine = Mesh(mesh.devices.reshape(SIZES), AXES)
    fsdp, tensor = AXES[:3], AXES[3:]
    placed = (
        P(fsdp + tensor, None),
        P(fsdp + tensor, None),
        P(None, None, tensor),
        P(tensor, None),
        P(fsdp, None, tensor),
        P(fsdp, None, tensor),
        P(),
    )
    return jax.shard_map(
        per_device,
        mesh=fine,
        in_specs=placed,
        out_specs=(P(fsdp, None, tensor), P(), P()),
        check_vma=False,
    )
```

```python
import jax
import jax.numpy as jnp
from jax import lax
from jax.experimental import pallas as pl
from jax.experimental.pallas import tpu as pltpu
from jax.sharding import Mesh, PartitionSpec as P

BF = jnp.bfloat16
F32 = jnp.float32
AXES = ("x_hi", "y", "core", "x_lo", "z")
SIZES = (2, 4, 2, 2, 8)


def swap(value, axis, step=1):
    size = lax.axis_size(axis)
    return lax.ppermute(value, axis, [(i, i ^ step) for i in range(size)])


def silu_parts(gate_pre):
    sigma_gate = jax.nn.sigmoid(gate_pre)
    silu_value = gate_pre * sigma_gate
    silu_slope = sigma_gate * (1.0 + gate_pre * (1.0 - sigma_gate))
    silu_curve = sigma_gate * (1.0 - sigma_gate) * (2.0 + gate_pre * (1.0 - 2.0 * sigma_gate))
    return (silu_value, silu_slope, silu_curve)


def neighbour(value):
    return lax.ppermute(value, "z", [(i, (i + 1) % 8 if i % 2 else (i - 1) % 8) for i in range(8)])


def by_pair(value):
    at = lax.axis_index("z") % 4
    return jnp.where((at == 1) | (at == 2), value[jnp.array([1, 0, 3, 2])], value[::-1])


def gather_z(block):
    half = block.shape[1] // 2
    even = jnp.stack([block] + [swap(block, "z", d) for d in (2, 4, 6)])
    odd = jnp.concatenate([swap(even[..., :half], "z"), by_pair(neighbour(even[..., half:]))], 2)
    return even, odd


def gather_x(even, odd):
    return jnp.concatenate([even, odd, swap(even, "x_lo"), swap(odd, "x_lo")], 0)


def fold_x(partial):
    rows, width = partial.shape
    halves = partial.reshape(2, 2, 4, rows // 16, width)
    other = swap(halves[1], "x_lo")
    return (halves[0].astype(F32) + other.astype(F32)).astype(BF)


def fold_z(folded):
    half = folded.shape[-1] // 2
    even, odd = folded[0], folded[1]
    other = jnp.concatenate([swap(odd[..., :half], "z"), by_pair(neighbour(odd[..., half:]))], 2)
    even = (even.astype(F32) + other.astype(F32)).astype(BF)
    total = even[0].astype(F32)
    for at in range(1, 4):
        total = total + swap(even[at], "z", 2 * at).astype(F32)
    return total


def dot(a, b, dims):
    return lax.dot_general(a, b, (dims, ((), ())), preferred_element_type=F32)


def add_blocks(index_ref, rows_ref, pieces, first, sums):
    at = first
    for piece in pieces:
        for block in range(piece.shape[2] // 256):
            start = pl.multiple_of(index_ref[at] * 256, 256)
            rows = rows_ref[:, pl.ds(start, 256)]
            for k in range(2):
                sums[k] = sums[k] + dot(piece[k, :, block * 256 : (block + 1) * 256], rows, ((1,), (1,)))
            at += 1


def near_kernel(index_ref, rows_ref, own_ref, other_ref, out_ref):
    sums = [0.0, 0.0]
    add_blocks(index_ref, rows_ref, (own_ref, other_ref), 0, sums)
    out_ref[0], out_ref[1] = sums


def far_kernel(index_ref, rows_ref, near_ref, projected_ref, *refs):
    pieces, (tangent_ref, act_ref) = refs[:8], refs[8:]
    sums = [near_ref[0], near_ref[1]]
    add_blocks(index_ref, rows_ref, pieces, 8, sums)
    tangent_ref[0], tangent_ref[1] = sums
    silu_value, silu_slope, _ = silu_parts(projected_ref[0])
    act = silu_slope * sums[0] * projected_ref[1] + silu_value * sums[1]
    act_ref[...] = act.astype(BF)


STEPS = 4


def by_step(arrays):
    return [
        pl.BlockSpec((2, a.shape[1] // STEPS, a.shape[2]), lambda i, index: (0, i, 0)) for a in arrays
    ]


def call_by_step(kernel, index, rows, arrays, out_shape, out_specs, bytes_accessed, flops):
    return pl.pallas_call(
        kernel,
        out_shape=out_shape,
        grid_spec=pltpu.PrefetchScalarGridSpec(
            num_scalar_prefetch=1,
            grid=(STEPS,),
            in_specs=[pl.BlockSpec(rows.shape, lambda i, index: (0, 0))] + by_step(arrays),
            out_specs=out_specs,
        ),
        compiler_params=pltpu.CompilerParams(vmem_limit_bytes=32 * 2**20),
        cost_estimate=pl.CostEstimate(flops=flops, bytes_accessed=bytes_accessed, transcendentals=0),
    )(index, rows, *arrays)


def total_over_devices(values):
    k = values.shape[0]
    tile = jnp.broadcast_to(jnp.pad(values, (0, 8 - k))[:, None], (8, 128))
    tile = tile + swap(tile, "core")
    for axes, size in (("z", 8), (("x_hi", "y", "x_lo"), 16)):
        sent = jnp.broadcast_to(tile[None], (size, 8, 128))
        tile = lax.all_to_all(sent, axes, 0, 0, tiled=True).sum(0)
    return tile[:k, 0]


def per_device(tokens, targets, gate_up, down_weight, direction, previous, beta_prev):
    width = tokens.shape[1]
    hidden = down_weight.shape[0]
    own_rows = direction.shape[0]
    token_total = tokens.shape[0] * 256
    gate_up_t = gate_up.transpose(1, 2, 0).reshape(2 * hidden, width)
    current_t = direction.transpose(1, 2, 0).reshape(2 * hidden, own_rows)
    earlier_t = previous.transpose(1, 2, 0).reshape(2 * hidden, own_rows)
    x_hi, y_at, core, x_lo, z_at = (lax.axis_index(n) for n in AXES)

    def owner(a, y, c):
        return ((x_hi ^ a) * 4 + y) * 2 + (core ^ c)

    index = jnp.stack(
        [owner(0, y, c) for c in range(2) for y in range(4)]
        + [owner(1, y_at ^ d, c) for d in range(4) for c in range(2)]
    )

    near = lax.all_gather(current_t, "y", axis=1, tiled=True)
    current_far = swap(current_t, "x_hi")

    even, odd = gather_z(tokens)
    even, odd, current_far = lax.optimization_barrier((even, odd, current_far))
    group_rows = gather_x(even, odd).reshape(-1, width)
    far = [current_far] + [swap(current_far, "y", d) for d in range(1, 4)]

    projected = dot(gate_up_t, group_rows, ((1,), (1,)))
    projected, near = lax.optimization_barrier((projected, near))
    gate_pre, up_pre = projected[:hidden], projected[hidden:]
    silu_value, silu_slope, silu_curve = silu_parts(gate_pre)
    hidden_act = (silu_value * up_pre).astype(BF)
    output_part = dot(hidden_act, down_weight, ((0,), (0,))).astype(BF)
    output_fold = fold_x(output_part)

    sent = tokens.reshape(-1, 16, own_rows).transpose(1, 0, 2)
    sent, _ = lax.optimization_barrier((sent, output_part))
    mine = lax.all_to_all(sent, AXES[:3], 0, 0, tiled=True)
    mine = lax.all_gather(mine, AXES[3:], axis=0)
    order = jnp.stack(
        [(x_lo ^ a) * 8 + (z_at ^ (2 * i + p)) for a in range(2) for p in range(2) for i in range(4)]
    )
    mine = mine[order].transpose(1, 0, 2, 3).reshape(2, 4, 2, -1, own_rows)

    def halves(value):
        return value.reshape(2, hidden, value.shape[1])

    chunk = hidden // STEPS
    near_pieces = [halves(near), halves(swap(near, "core"))]
    count = group_rows.shape[0]
    sum_spec = pl.BlockSpec((2, chunk, count), lambda i, index: (0, i, 0))
    sum_shape = jax.ShapeDtypeStruct((2, hidden, count), F32)
    flops = 2 * hidden * width * count
    near_sums = call_by_step(
        near_kernel, index, group_rows, near_pieces, sum_shape, sum_spec, hidden * width * 2, flops
    )
    far_pieces = [halves(p) for piece in far for p in (piece, swap(piece, "core"))]
    tangent, tangent_act = call_by_step(
        far_kernel,
        index,
        group_rows,
        [near_sums, halves(projected)] + far_pieces,
        (sum_shape, jax.ShapeDtypeStruct((hidden, count), BF)),
        (sum_spec, pl.BlockSpec((chunk, count), lambda i, index: (i, 0))),
        hidden * width * 2,
        flops,
    )
    tangent_gate, tangent_up = tangent[0], tangent[1]
    tangent_part = dot(tangent_act, down_weight, ((0,), (0,))).astype(BF)
    tangent_fold = fold_x(tangent_part)
    output_sum = fold_z(output_fold)
    tangent_sum = fold_z(tangent_fold)
    error_rows = ((output_sum - targets.astype(F32)) / token_total).astype(BF)
    tangent_error = (tangent_sum / token_total).astype(BF)
    errors = jnp.concatenate([error_rows, tangent_error], 0)
    errors = gather_x(*gather_z(errors)).reshape(16, 2, -1, width)
    back_error = dot(down_weight, errors[:, 0].reshape(-1, width), ((1,), (1,)))
    back_tangent = dot(down_weight, errors[:, 1].reshape(-1, width), ((1,), (1,)))

    grad_gate = back_tangent * up_pre * silu_slope + back_error * (
        tangent_up * silu_slope + up_pre * silu_curve * tangent_gate
    )
    grad_up = back_tangent * silu_value + back_error * silu_slope * tangent_gate
    tangent_grad = jnp.concatenate([grad_gate, grad_up], 0).astype(BF)
    grad_far = swap(tangent_grad, "x_hi")
    curvature = 0.0
    for a, piece in enumerate((tangent_grad, grad_far)):
        piece = lax.all_gather(piece, "y", axis=1, tiled=True)
        for c, block in enumerate((piece, swap(piece, "core"))):
            there = lax.dynamic_index_in_dim(mine, x_hi ^ a, 0, keepdims=False)
            there = lax.dynamic_index_in_dim(there, core ^ c, 1, keepdims=False)
            curvature = curvature + dot(block, there.reshape(-1, own_rows), ((1,), (0,)))

    current = current_t.astype(F32)
    shifted = curvature - beta_prev * earlier_t.astype(F32)
    sums = total_over_devices(
        jnp.stack(
            [
                jnp.sum(curvature * current),
                jnp.sum(shifted * shifted),
                jnp.sum(shifted * current),
                jnp.sum(current * current),
            ]
        )
    )
    entry_count = 2 * own_rows * hidden * 256
    rayleigh = sums[0] / entry_count
    square = (sums[1] - 2.0 * rayleigh * sums[2] + rayleigh * rayleigh * sums[3]) / entry_count
    offdiagonal = jnp.sqrt(jnp.maximum(square, 0.0) + 1e-06)
    new_direction = ((shifted - rayleigh * current) / offdiagonal).astype(BF)
    new_direction = new_direction.reshape(2, hidden, own_rows).transpose(2, 0, 1)
    return (new_direction, rayleigh, offdiagonal)


def solution(mesh):
    fine = Mesh(mesh.devices.reshape(SIZES), AXES)
    fsdp, tensor = AXES[:3], AXES[3:]
    placed = (
        P(fsdp + tensor, None),
        P(fsdp + tensor, None),
        P(None, None, tensor),
        P(tensor, None),
        P(fsdp, None, tensor),
        P(fsdp, None, tensor),
        P(),
    )
    return jax.shard_map(
        per_device,
        mesh=fine,
        in_specs=placed,
        out_specs=(P(fsdp, None, tensor), P(), P()),
        check_vma=False,
    )
```

```python
import jax
import jax.numpy as jnp
from jax import lax
from jax.experimental import pallas as pl
from jax.experimental.pallas import tpu as pltpu
from jax.sharding import Mesh, PartitionSpec as P

BF = jnp.bfloat16
F32 = jnp.float32
AXES = ("x_hi", "y", "core", "x_lo", "z")
SIZES = (2, 4, 2, 2, 8)


def swap(value, axis, step=1):
    size = lax.axis_size(axis)
    return lax.ppermute(value, axis, [(i, i ^ step) for i in range(size)])


def silu_parts(gate_pre):
    sigma_gate = jax.nn.sigmoid(gate_pre)
    silu_value = gate_pre * sigma_gate
    silu_slope = sigma_gate * (1.0 + gate_pre * (1.0 - sigma_gate))
    silu_curve = sigma_gate * (1.0 - sigma_gate) * (2.0 + gate_pre * (1.0 - 2.0 * sigma_gate))
    return (silu_value, silu_slope, silu_curve)


def neighbour(value):
    return lax.ppermute(value, "z", [(i, (i + 1) % 8 if i % 2 else (i - 1) % 8) for i in range(8)])


def by_pair(value):
    at = lax.axis_index("z") % 4
    return jnp.where((at == 1) | (at == 2), value[jnp.array([1, 0, 3, 2])], value[::-1])


def gather_even(block):
    return jnp.stack([block] + [swap(block, "z", d) for d in (2, 4, 6)])


def gather_z(even):
    half = even.shape[2] // 2
    odd = jnp.concatenate([swap(even[..., :half], "z"), by_pair(neighbour(even[..., half:]))], 2)
    return even, odd


def gather_x(even, odd):
    return jnp.concatenate([even, odd, swap(even, "x_lo"), swap(odd, "x_lo")], 0)


def fold_x(partial):
    rows, width = partial.shape
    halves = partial.reshape(2, 2, 4, rows // 16, width)
    other = swap(halves[1], "x_lo")
    return (halves[0].astype(F32) + other.astype(F32)).astype(BF)


def fold_z(folded):
    half = folded.shape[-1] // 2
    even, odd = folded[0], folded[1]
    other = jnp.concatenate([swap(odd[..., :half], "z"), by_pair(neighbour(odd[..., half:]))], 2)
    even = (even.astype(F32) + other.astype(F32)).astype(BF)
    total = even[0].astype(F32)
    for at in range(1, 4):
        total = total + swap(even[at], "z", 2 * at).astype(F32)
    return total


def dot(a, b, dims):
    return lax.dot_general(a, b, (dims, ((), ())), preferred_element_type=F32)


def tangent_kernel(first, index_ref, rows_ref, other_ref, pieces_ref, *refs):
    before, outs = refs[:first], refs[first:]
    for k in range(2):
        total = before[0][k] if before else 0.0
        for at in range(4):
            start = pl.multiple_of(index_ref[4 * first + at] * 256, 256)
            rows = jnp.concatenate([ref[:, pl.ds(start, 256)] for ref in (rows_ref, other_ref)], 0)
            total = total + dot(pieces_ref[at, k], rows, ((1,), (1,)))
        width = outs[0].shape[2]
        for at, out in enumerate(outs):
            out[k] = total[:, at * width : (at + 1) * width]


def act_kernel(projected_ref, own_ref, other_ref, tangent_ref, act_ref):
    gate, up = [own_ref[k] + other_ref[k] for k in range(2)]
    tangent_ref[0], tangent_ref[1] = gate, up
    silu_value, silu_slope, _ = silu_parts(projected_ref[0])
    act_ref[...] = (silu_slope * gate * projected_ref[1] + silu_value * up).astype(BF)


STEPS = 4


def tangent_call(first, index, rows, pieces, before, out_shape):
    hidden = pieces.shape[2]
    chunk = hidden // STEPS

    def spec(size):
        return pl.BlockSpec((2, chunk, size), lambda i, index: (0, i, 0))

    return pl.pallas_call(
        lambda *refs: tangent_kernel(first, *refs),
        out_shape=out_shape,
        grid_spec=pltpu.PrefetchScalarGridSpec(
            num_scalar_prefetch=1,
            grid=(STEPS,),
            in_specs=[pl.BlockSpec(r.shape, lambda i, index: (0, 0)) for r in rows]
            + [pl.BlockSpec((4, 2, chunk, pieces.shape[3]), lambda i, index: (0, 0, i, 0))]
            + [spec(b.shape[2]) for b in before],
            out_specs=[spec(o.shape[2]) for o in out_shape],
        ),
        compiler_params=pltpu.CompilerParams(vmem_limit_bytes=32 * 2**20),
        cost_estimate=pl.CostEstimate(
            flops=8 * hidden * pieces.shape[3] * rows[0].shape[0] * 4,
            bytes_accessed=pieces.size * 2,
            transcendentals=0,
        ),
    )(index, *rows, pieces, *before)


def curvature_kernel(index_ref, beta_ref, columns_ref, *refs):
    blocks, (current_ref, earlier_ref, shifted_ref, sums_ref) = refs[:4], refs[4:]
    curvature = 0.0
    for at, block in enumerate(blocks):
        rows = jnp.concatenate([columns_ref[index_ref[4 * at + y]] for y in range(4)], 0)
        grads = jnp.concatenate([block[y] for y in range(4)], 1)
        curvature = curvature + dot(grads, rows, ((1,), (0,)))
    current = current_ref[...].astype(F32)
    shifted = curvature - beta_ref[0, 0] * earlier_ref[...].astype(F32)
    shifted_ref[...] = shifted

    def row(product):
        lanes = jnp.sum(product, 0, keepdims=True)
        return lanes[:, :128] + lanes[:, 128:]

    @pl.when(pl.program_id(0) == 0)
    def _():
        sums_ref[...] = jnp.zeros_like(sums_ref)

    parts = [row(p) for p in (curvature * current, shifted * shifted, shifted * current, current * current)]
    sums_ref[...] += jnp.concatenate(parts + [jnp.zeros((4, 128), F32)], 0)


def scale_kernel(entry_count, sums_ref, shifted_ref, current_ref, out_ref, rayleigh_ref, offdiagonal_ref):
    sums = jnp.sum(jnp.sum(sums_ref[...], 0), 1, keepdims=True)
    inner, square, mixed, norm = [sums[k : k + 1] for k in range(4)]
    rayleigh = inner / entry_count
    square = (square - 2.0 * rayleigh * mixed + rayleigh * rayleigh * norm) / entry_count
    offdiagonal = jnp.sqrt(jnp.maximum(square, 0.0) + 1e-06)
    rayleigh_ref[...] = jnp.broadcast_to(rayleigh, rayleigh_ref.shape)
    offdiagonal_ref[...] = jnp.broadcast_to(offdiagonal, offdiagonal_ref.shape)
    residual = shifted_ref[...] - rayleigh * current_ref[...].astype(F32)
    out_ref[...] = (residual / offdiagonal).astype(BF)


def per_device(tokens, targets, gate_up, down_weight, direction, previous, beta_prev):
    width = tokens.shape[1]
    hidden = down_weight.shape[0]
    own_rows = direction.shape[0]
    token_total = tokens.shape[0] * 256
    gate_up_t = gate_up.transpose(1, 2, 0).reshape(2 * hidden, width)
    current_t = direction.transpose(1, 2, 0).reshape(2 * hidden, own_rows)
    earlier_t = previous.transpose(1, 2, 0).reshape(2 * hidden, own_rows)
    x_hi, y_at, core, x_lo, z_at = (lax.axis_index(n) for n in AXES)

    def owner(a, y, c):
        return ((x_hi ^ a) * 4 + y) * 2 + (core ^ c)

    index = jnp.stack([owner(0, y, 0) for y in range(4)] + [owner(1, y, 0) for y in range(4)])

    current_far = swap(current_t, "x_hi")
    near = lax.all_gather(current_t, "y")
    far = lax.all_gather(current_far, "y")

    even, current_far = lax.optimization_barrier((gather_even(tokens), current_far))
    group_rows = gather_x(*gather_z(even)).reshape(-1, width)
    other_rows = swap(group_rows, "core")

    projected = dot(gate_up_t, group_rows, ((1,), (1,)))
    projected, near = lax.optimization_barrier((projected, near))
    gate_pre, up_pre = projected[:hidden], projected[hidden:]
    silu_value, silu_slope, silu_curve = silu_parts(gate_pre)
    hidden_act = (silu_value * up_pre).astype(BF)
    output_part = dot(hidden_act, down_weight, ((0,), (0,))).astype(BF)
    output_fold = fold_x(output_part)

    def cut(value, start, size):
        return lax.dynamic_slice_in_dim(value, start * own_rows, size * own_rows, value.ndim - 1)

    both = jnp.stack([cut(group_rows, x_hi * 8, 8), swap(cut(group_rows, 8 - x_hi * 8, 8), "x_hi")])

    def halves(value):
        return value.reshape(2, hidden, value.shape[1])

    chunk = hidden // STEPS
    count = group_rows.shape[0]

    def sum_of(size):
        return jax.ShapeDtypeStruct((2, hidden, size), F32)

    own_shape = sum_of(count)
    rows_pair = (group_rows, other_rows)
    near_sums = tangent_call(0, index, rows_pair, near.reshape(4, 2, hidden, -1), [], [sum_of(2 * count)])
    own_sums, other_sums = tangent_call(
        1, index, rows_pair, far.reshape(4, 2, hidden, -1), near_sums, [own_shape, own_shape]
    )
    step_spec = pl.BlockSpec((2, chunk, count), lambda i: (0, i, 0))
    tangent, tangent_act = pl.pallas_call(
        act_kernel,
        out_shape=(own_shape, jax.ShapeDtypeStruct((hidden, count), BF)),
        grid=(STEPS,),
        in_specs=[step_spec] * 3,
        out_specs=(step_spec, pl.BlockSpec((chunk, count), lambda i: (i, 0))),
        compiler_params=pltpu.CompilerParams(vmem_limit_bytes=32 * 2**20),
        cost_estimate=pl.CostEstimate(flops=2**20, bytes_accessed=2 * 2**20, transcendentals=2**16),
    )(halves(projected), own_sums, swap(other_sums, "core"))
    tangent_gate, tangent_up = tangent[0], tangent[1]
    tangent_part = dot(tangent_act, down_weight, ((0,), (0,))).astype(BF)
    tangent_fold = fold_x(tangent_part)


    output_sum = fold_z(output_fold)
    tangent_sum = fold_z(tangent_fold)
    error_rows = ((output_sum - targets.astype(F32)) / token_total).astype(BF)
    tangent_error = (tangent_sum / token_total).astype(BF)
    errors = jnp.concatenate([error_rows, tangent_error], 0)
    errors, both = lax.optimization_barrier((errors, both))
    own_columns = jnp.stack(
        [cut(both, y_at * 2, 2)] + [swap(cut(both, (y_at ^ d) * 2, 2), "y", d) for d in range(1, 4)], 1
    )
    own_columns = jnp.stack(
        [cut(own_columns, core, 1), swap(cut(own_columns, 1 - core, 1), "core")], 1
    ).reshape(16, count, own_rows)
    errors = gather_x(*gather_z(gather_even(errors))).reshape(16, 2, -1, width)
    back_error = dot(down_weight, errors[:, 0].reshape(-1, width), ((1,), (1,)))
    back_tangent = dot(down_weight, errors[:, 1].reshape(-1, width), ((1,), (1,)))

    grad_gate = back_tangent * up_pre * silu_slope + back_error * (
        tangent_up * silu_slope + up_pre * silu_curve * tangent_gate
    )
    grad_up = back_tangent * silu_value + back_error * silu_slope * tangent_gate
    tangent_grad = jnp.concatenate([grad_gate, grad_up], 0).astype(BF)
    grad_far = swap(tangent_grad, "x_hi")
    blocks = []
    for piece in (tangent_grad, grad_far):
        piece = lax.all_gather(piece, "y")
        blocks += [piece, swap(piece, "core")]
    groups = jnp.stack([(a * 2 + c) * 4 + (y_at ^ y) for a in range(2) for c in range(2) for y in range(4)])
    rows = 2 * hidden // STEPS
    row_spec = pl.BlockSpec((rows, own_rows), lambda i, index: (i, 0))
    shifted, sums = pl.pallas_call(
        curvature_kernel,
        out_shape=(
            jax.ShapeDtypeStruct((2 * hidden, own_rows), F32),
            jax.ShapeDtypeStruct((8, 128), F32),
        ),
        grid_spec=pltpu.PrefetchScalarGridSpec(
            num_scalar_prefetch=1,
            grid=(STEPS,),
            in_specs=[
                pl.BlockSpec(memory_space=pltpu.SMEM),
                pl.BlockSpec(own_columns.shape, lambda i, index: (0, 0, 0)),
            ]
            + [pl.BlockSpec((4, rows, count), lambda i, index: (0, i, 0))] * 4
            + [row_spec] * 2,
            out_specs=(row_spec, pl.BlockSpec((8, 128), lambda i, index: (0, 0))),
        ),
        compiler_params=pltpu.CompilerParams(vmem_limit_bytes=32 * 2**20),
        cost_estimate=pl.CostEstimate(flops=2**30, bytes_accessed=7 * 2**20, transcendentals=0),
    )(groups, beta_prev.reshape(1, 1), own_columns, *blocks, current_t, earlier_t)

    for axes in (("z",), AXES[:4]):
        size = lax.axis_size(axes)
        if axes != ("z",):
            sums = sums.sum(0)
        sums = lax.all_to_all(jnp.broadcast_to(sums[None], (size, 8, 128)), axes, 0, 0, tiled=True)

    row_spec = pl.BlockSpec((rows, own_rows), lambda i: (i, 0))
    one_spec = pl.BlockSpec((1, 128), lambda i: (0, 0))
    new_direction, rayleigh, offdiagonal = pl.pallas_call(
        lambda *refs: scale_kernel(2 * own_rows * hidden * 256, *refs),
        out_shape=(
            jax.ShapeDtypeStruct((2 * hidden, own_rows), BF),
            jax.ShapeDtypeStruct((1, 128), F32),
            jax.ShapeDtypeStruct((1, 128), F32),
        ),
        grid=(STEPS,),
        in_specs=[pl.BlockSpec(sums.shape, lambda i: (0, 0, 0)), row_spec, row_spec],
        out_specs=(row_spec, one_spec, one_spec),
        compiler_params=pltpu.CompilerParams(vmem_limit_bytes=32 * 2**20),
        cost_estimate=pl.CostEstimate(flops=2**20, bytes_accessed=2 * 2**20, transcendentals=0),
    )(sums, shifted, current_t)
    rayleigh, offdiagonal = rayleigh[0, 0], offdiagonal[0, 0]
    new_direction = new_direction.reshape(2, hidden, own_rows).transpose(2, 0, 1)
    return (new_direction, rayleigh, offdiagonal)


def solution(mesh):
    fine = Mesh(mesh.devices.reshape(SIZES), AXES)
    fsdp, tensor = AXES[:3], AXES[3:]
    placed = (
        P(fsdp + tensor, None),
        P(fsdp + tensor, None),
        P(None, None, tensor),
        P(tensor, None),
        P(fsdp, None, tensor),
        P(fsdp, None, tensor),
        P(),
    )
    return jax.shard_map(
        per_device,
        mesh=fine,
        in_specs=placed,
        out_specs=(P(fsdp, None, tensor), P(), P()),
        check_vma=False,
    )
```

```python
import jax
import jax.numpy as jnp
from jax import lax
from jax.experimental import pallas as pl
from jax.experimental.pallas import tpu as pltpu
from jax.sharding import Mesh, PartitionSpec as P

BF = jnp.bfloat16
F32 = jnp.float32
AXES = ("x_hi", "y", "core", "x_lo", "z")
SIZES = (2, 4, 2, 2, 8)


def swap(value, axis, step=1):
    size = lax.axis_size(axis)
    return lax.ppermute(value, axis, [(i, i ^ step) for i in range(size)])


def silu_parts(gate_pre):
    sigma_gate = jax.nn.sigmoid(gate_pre)
    silu_value = gate_pre * sigma_gate
    silu_slope = sigma_gate * (1.0 + gate_pre * (1.0 - sigma_gate))
    silu_curve = sigma_gate * (1.0 - sigma_gate) * (2.0 + gate_pre * (1.0 - 2.0 * sigma_gate))
    return (silu_value, silu_slope, silu_curve)


def neighbour(value):
    return lax.ppermute(value, "z", [(i, (i + 1) % 8 if i % 2 else (i - 1) % 8) for i in range(8)])


def by_pair(value):
    at = lax.axis_index("z") % 4
    return jnp.where((at == 1) | (at == 2), value[jnp.array([1, 0, 3, 2])], value[::-1])


def gather_even(block):
    return jnp.stack([block] + [swap(block, "z", d) for d in (2, 4, 6)])


def gather_z(even):
    half = even.shape[2] // 2
    odd = jnp.concatenate([swap(even[..., :half], "z"), by_pair(neighbour(even[..., half:]))], 2)
    return even, odd


def gather_x(even, odd):
    return jnp.concatenate([even, odd, swap(even, "x_lo"), swap(odd, "x_lo")], 0)


def fold_x(partial):
    rows, width = partial.shape
    halves = partial.reshape(2, 2, 4, rows // 16, width)
    other = swap(halves[1], "x_lo")
    return (halves[0].astype(F32) + other.astype(F32)).astype(BF)


def fold_z(folded):
    half = folded.shape[-1] // 2
    even, odd = folded[0], folded[1]
    other = jnp.concatenate([swap(odd[..., :half], "z"), by_pair(neighbour(odd[..., half:]))], 2)
    even = (even.astype(F32) + other.astype(F32)).astype(BF)
    total = even[0].astype(F32)
    for at in range(1, 4):
        total = total + swap(even[at], "z", 2 * at).astype(F32)
    return total


def dot(a, b, dims):
    return lax.dot_general(a, b, (dims, ((), ())), preferred_element_type=F32)


def tangent_kernel(first, index_ref, rows_ref, other_ref, *refs):
    if first:
        pieces, before_ref, outs = refs[:4], refs[4], refs[5:]
        at = 4
    else:
        pieces_ref, before_ref, outs = refs[0], None, refs[1:]
        at = 0
    for k in range(2):
        if first:
            blocks = [pieces[2 * k + i // 2][i % 2] for i in range(4)]
        else:
            blocks = [pieces_ref[i, k] for i in range(4)]
            at = 0
        total = before_ref[k] if first else 0.0
        for block in blocks:
            start = pl.multiple_of(index_ref[at] * 256, 256)
            rows = jnp.concatenate([ref[:, pl.ds(start, 256)] for ref in (rows_ref, other_ref)], 0)
            total = total + dot(block, rows, ((1,), (1,)))
            at += 1
        width = outs[0].shape[2]
        for place, out in enumerate(outs):
            out[k] = total[:, place * width : (place + 1) * width]


def act_kernel(projected_ref, own_ref, other_ref, tangent_ref, act_ref):
    gate, up = [own_ref[k] + other_ref[k] for k in range(2)]
    tangent_ref[0], tangent_ref[1] = gate, up
    silu_value, silu_slope, _ = silu_parts(projected_ref[0])
    act_ref[...] = (silu_slope * gate * projected_ref[1] + silu_value * up).astype(BF)


STEPS = 4


def tangent_call(first, index, rows, pieces, before, out_shape):
    hidden, depth = pieces[0].shape[-2:]
    chunk = hidden // STEPS

    def spec(size):
        return pl.BlockSpec((2, chunk, size), lambda i, index: (0, i, 0))

    if first:
        piece_specs = [spec(depth)] * 4
    else:
        piece_specs = [pl.BlockSpec((4, 2, chunk, depth), lambda i, index: (0, 0, i, 0))]
    return pl.pallas_call(
        lambda *refs: tangent_kernel(first, *refs),
        out_shape=out_shape,
        grid_spec=pltpu.PrefetchScalarGridSpec(
            num_scalar_prefetch=1,
            grid=(STEPS,),
            in_specs=[pl.BlockSpec(r.shape, lambda i, index: (0, 0)) for r in rows]
            + piece_specs
            + [spec(b.shape[2]) for b in before],
            out_specs=[spec(o.shape[2]) for o in out_shape],
        ),
        compiler_params=pltpu.CompilerParams(vmem_limit_bytes=32 * 2**20),
        cost_estimate=pl.CostEstimate(
            flops=8 * hidden * depth * rows[0].shape[0] * 4,
            bytes_accessed=16 * hidden * depth,
            transcendentals=0,
        ),
    )(index, *rows, *pieces, *before)


def curvature_kernel(index_ref, beta_ref, columns_ref, *refs):
    blocks, (current_ref, earlier_ref, shifted_ref, sums_ref) = refs[:4], refs[4:]
    curvature = 0.0
    for at, block in enumerate(blocks):
        rows = jnp.concatenate([columns_ref[index_ref[4 * at + y]] for y in range(4)], 0)
        grads = jnp.concatenate([block[y] for y in range(4)], 1)
        curvature = curvature + dot(grads, rows, ((1,), (0,)))
    current = current_ref[...].astype(F32)
    shifted = curvature - beta_ref[0, 0] * earlier_ref[...].astype(F32)
    shifted_ref[...] = shifted

    def row(product):
        lanes = jnp.sum(product, 0, keepdims=True)
        return lanes[:, :128] + lanes[:, 128:]

    @pl.when(pl.program_id(0) == 0)
    def _():
        sums_ref[...] = jnp.zeros_like(sums_ref)

    parts = [row(p) for p in (curvature * current, shifted * shifted, shifted * current, current * current)]
    sums_ref[...] += jnp.concatenate(parts + [jnp.zeros((4, 128), F32)], 0)


def scale_kernel(entry_count, sums_ref, shifted_ref, current_ref, out_ref, rayleigh_ref, offdiagonal_ref):
    sums = jnp.sum(jnp.sum(sums_ref[...], 0), 1, keepdims=True)
    inner, square, mixed, norm = [sums[k : k + 1] for k in range(4)]
    rayleigh = inner / entry_count
    square = (square - 2.0 * rayleigh * mixed + rayleigh * rayleigh * norm) / entry_count
    offdiagonal = jnp.sqrt(jnp.maximum(square, 0.0) + 1e-06)
    rayleigh_ref[...] = jnp.broadcast_to(rayleigh, rayleigh_ref.shape)
    offdiagonal_ref[...] = jnp.broadcast_to(offdiagonal, offdiagonal_ref.shape)
    residual = shifted_ref[...] - rayleigh * current_ref[...].astype(F32)
    out_ref[...] = (residual / offdiagonal).astype(BF)


def per_device(tokens, targets, gate_up, down_weight, direction, previous, beta_prev):
    width = tokens.shape[1]
    hidden = down_weight.shape[0]
    own_rows = direction.shape[0]
    token_total = tokens.shape[0] * 256
    gate_up_t = gate_up.transpose(1, 2, 0).reshape(2 * hidden, width)
    current_t = direction.transpose(1, 2, 0).reshape(2 * hidden, own_rows)
    earlier_t = previous.transpose(1, 2, 0).reshape(2 * hidden, own_rows)
    x_hi, y_at, core, x_lo, z_at = (lax.axis_index(n) for n in AXES)

    def owner(a, y, c):
        return ((x_hi ^ a) * 4 + y) * 2 + (core ^ c)

    index = jnp.stack([owner(0, y, 0) for y in range(4)] + [owner(1, y_at ^ d, 0) for d in (0, 1, 3, 2, 0, 3, 1, 2)])

    current_far = swap(current_t, "x_hi")
    near = lax.all_gather(current_t, "y")

    even, current_far = lax.optimization_barrier((gather_even(tokens), current_far))
    far = []
    for rows, step in ((current_far[:hidden], 1), (current_far[hidden:], 3)):
        pair = jnp.stack([rows, swap(rows, "y", step)])
        far += [pair, swap(pair, "y", 4 - step)]
    group_rows = gather_x(*gather_z(even)).reshape(-1, width)
    other_rows = swap(group_rows, "core")

    projected = dot(gate_up_t, group_rows, ((1,), (1,)))
    projected, near = lax.optimization_barrier((projected, near))
    gate_pre, up_pre = projected[:hidden], projected[hidden:]
    silu_value, silu_slope, silu_curve = silu_parts(gate_pre)
    hidden_act = (silu_value * up_pre).astype(BF)
    output_part = dot(hidden_act, down_weight, ((0,), (0,))).astype(BF)
    def cut(value, start, size):
        return lax.dynamic_slice_in_dim(value, start * own_rows, size * own_rows, value.ndim - 1)

    both = jnp.stack([cut(group_rows, x_hi * 8, 8), swap(cut(group_rows, 8 - x_hi * 8, 8), "x_hi")])

    output_part, both, *far = lax.optimization_barrier((output_part, both, *far))
    output_fold = fold_x(output_part)

    def halves(value):
        return value.reshape(2, hidden, value.shape[1])

    chunk = hidden // STEPS
    count = group_rows.shape[0]

    def sum_of(size):
        return jax.ShapeDtypeStruct((2, hidden, size), F32)

    own_shape = sum_of(count)
    rows_pair = (group_rows, other_rows)
    near_sums = tangent_call(0, index, rows_pair, [near.reshape(4, 2, hidden, -1)], [], [sum_of(2 * count)])
    own_sums, other_sums = tangent_call(
        1, index, rows_pair, far, near_sums, [own_shape, own_shape]
    )
    own_sums, output_fold = lax.optimization_barrier((own_sums, output_fold))
    step_spec = pl.BlockSpec((2, chunk, count), lambda i: (0, i, 0))
    tangent, tangent_act = pl.pallas_call(
        act_kernel,
        out_shape=(own_shape, jax.ShapeDtypeStruct((hidden, count), BF)),
        grid=(STEPS,),
        in_specs=[step_spec] * 3,
        out_specs=(step_spec, pl.BlockSpec((chunk, count), lambda i: (i, 0))),
        compiler_params=pltpu.CompilerParams(vmem_limit_bytes=32 * 2**20),
        cost_estimate=pl.CostEstimate(flops=2**20, bytes_accessed=2 * 2**20, transcendentals=2**16),
    )(halves(projected), own_sums, swap(other_sums, "core"))
    tangent_gate, tangent_up = tangent[0], tangent[1]
    tangent_part = dot(tangent_act, down_weight, ((0,), (0,))).astype(BF)
    tangent_fold = fold_x(tangent_part)


    sums = fold_z(jnp.concatenate([output_fold, tangent_fold], 2))
    output_sum, tangent_sum = sums[: targets.shape[0]], sums[targets.shape[0] :]
    error_rows = ((output_sum - targets.astype(F32)) / token_total).astype(BF)
    tangent_error = (tangent_sum / token_total).astype(BF)
    errors = jnp.concatenate([error_rows, tangent_error], 0)
    errors, both = lax.optimization_barrier((errors, both))
    own_columns = jnp.stack(
        [cut(both, y_at * 2, 2)] + [swap(cut(both, (y_at ^ d) * 2, 2), "y", d) for d in range(1, 4)], 1
    )
    own_columns = jnp.stack(
        [cut(own_columns, core, 1), swap(cut(own_columns, 1 - core, 1), "core")], 1
    ).reshape(16, count, own_rows)
    errors = gather_x(*gather_z(gather_even(errors))).reshape(16, 2, -1, width)
    back_error = dot(down_weight, errors[:, 0].reshape(-1, width), ((1,), (1,)))
    back_tangent = dot(down_weight, errors[:, 1].reshape(-1, width), ((1,), (1,)))

    grad_gate = back_tangent * up_pre * silu_slope + back_error * (
        tangent_up * silu_slope + up_pre * silu_curve * tangent_gate
    )
    grad_up = back_tangent * silu_value + back_error * silu_slope * tangent_gate
    tangent_grad = jnp.concatenate([grad_gate, grad_up], 0).astype(BF)
    tangent_grad, own_columns = lax.optimization_barrier((tangent_grad, own_columns))
    grad_far = swap(tangent_grad, "x_hi")
    blocks = []
    for piece in (tangent_grad, grad_far):
        piece = lax.all_gather(piece, "y")
        blocks += [piece, swap(piece, "core")]
    groups = jnp.stack([(a * 2 + c) * 4 + (y_at ^ y) for a in range(2) for c in range(2) for y in range(4)])
    rows = 2 * hidden // STEPS
    row_spec = pl.BlockSpec((rows, own_rows), lambda i, index: (i, 0))
    shifted, sums = pl.pallas_call(
        curvature_kernel,
        out_shape=(
            jax.ShapeDtypeStruct((2 * hidden, own_rows), F32),
            jax.ShapeDtypeStruct((8, 128), F32),
        ),
        grid_spec=pltpu.PrefetchScalarGridSpec(
            num_scalar_prefetch=1,
            grid=(STEPS,),
            in_specs=[
                pl.BlockSpec(memory_space=pltpu.SMEM),
                pl.BlockSpec(own_columns.shape, lambda i, index: (0, 0, 0)),
            ]
            + [pl.BlockSpec((4, rows, count), lambda i, index: (0, i, 0))] * 4
            + [row_spec] * 2,
            out_specs=(row_spec, pl.BlockSpec((8, 128), lambda i, index: (0, 0))),
        ),
        compiler_params=pltpu.CompilerParams(vmem_limit_bytes=32 * 2**20),
        cost_estimate=pl.CostEstimate(flops=2**30, bytes_accessed=7 * 2**20, transcendentals=0),
    )(groups, beta_prev.reshape(1, 1), own_columns, *blocks, current_t, earlier_t)

    for axes in (("z",), AXES[:4]):
        size = lax.axis_size(axes)
        if axes != ("z",):
            sums = sums.sum(0)
        sums = lax.all_to_all(jnp.broadcast_to(sums[None], (size, 8, 128)), axes, 0, 0, tiled=True)

    row_spec = pl.BlockSpec((rows, own_rows), lambda i: (i, 0))
    one_spec = pl.BlockSpec((1, 128), lambda i: (0, 0))
    new_direction, rayleigh, offdiagonal = pl.pallas_call(
        lambda *refs: scale_kernel(2 * own_rows * hidden * 256, *refs),
        out_shape=(
            jax.ShapeDtypeStruct((2 * hidden, own_rows), BF),
            jax.ShapeDtypeStruct((1, 128), F32),
            jax.ShapeDtypeStruct((1, 128), F32),
        ),
        grid=(STEPS,),
        in_specs=[pl.BlockSpec(sums.shape, lambda i: (0, 0, 0)), row_spec, row_spec],
        out_specs=(row_spec, one_spec, one_spec),
        compiler_params=pltpu.CompilerParams(vmem_limit_bytes=32 * 2**20),
        cost_estimate=pl.CostEstimate(flops=2**20, bytes_accessed=2 * 2**20, transcendentals=0),
    )(sums, shifted, current_t)
    rayleigh, offdiagonal = rayleigh[0, 0], offdiagonal[0, 0]
    new_direction = new_direction.reshape(2, hidden, own_rows).transpose(2, 0, 1)
    return (new_direction, rayleigh, offdiagonal)


def solution(mesh):
    fine = Mesh(mesh.devices.reshape(SIZES), AXES)
    fsdp, tensor = AXES[:3], AXES[3:]
    placed = (
        P(fsdp + tensor, None),
        P(fsdp + tensor, None),
        P(None, None, tensor),
        P(tensor, None),
        P(fsdp, None, tensor),
        P(fsdp, None, tensor),
        P(),
    )
    return jax.shard_map(
        per_device,
        mesh=fine,
        in_specs=placed,
        out_specs=(P(fsdp, None, tensor), P(), P()),
        check_vma=False,
    )
```

```python
import jax
import jax.numpy as jnp
from jax import lax
from jax.experimental import pallas as pl
from jax.experimental.pallas import tpu as pltpu
from jax.sharding import Mesh, PartitionSpec as P

BF = jnp.bfloat16
F32 = jnp.float32
AXES = ("x_hi", "y", "core", "x_lo", "z")
SIZES = (2, 4, 2, 2, 8)


def swap(value, axis, step=1):
    size = lax.axis_size(axis)
    return lax.ppermute(value, axis, [(i, i ^ step) for i in range(size)])


def silu_parts(gate_pre):
    sigma_gate = jax.nn.sigmoid(gate_pre)
    silu_value = gate_pre * sigma_gate
    silu_slope = sigma_gate * (1.0 + gate_pre * (1.0 - sigma_gate))
    silu_curve = sigma_gate * (1.0 - sigma_gate) * (2.0 + gate_pre * (1.0 - 2.0 * sigma_gate))
    return (silu_value, silu_slope, silu_curve)


def neighbour(value):
    return lax.ppermute(value, "z", [(i, (i + 1) % 8 if i % 2 else (i - 1) % 8) for i in range(8)])


def by_pair(value):
    at = lax.axis_index("z") % 4
    pairs = value.reshape(2, 2, *value.shape[1:])
    turned = jnp.where((at == 1) | (at == 2), lax.rev(pairs, (1,)), lax.rev(pairs, (0, 1)))
    return turned.reshape(value.shape)


def gather_even(block):
    return jnp.stack([block] + [swap(block, "z", d) for d in (2, 4, 6)])


def gather_z(even):
    half = even.shape[2] // 2
    odd = jnp.concatenate([swap(even[..., :half], "z"), by_pair(neighbour(even[..., half:]))], 2)
    return even, odd


def gather_x(even, odd):
    return jnp.concatenate([even, odd, swap(even, "x_lo"), swap(odd, "x_lo")], 0)


def gather_both(block):
    half = block.shape[1] // 2
    rest = [swap(block, "z", d) for d in (2, 4, 6)]
    across = swap(block, "x_lo")[None]
    near = jnp.stack([block] + rest)
    across = jnp.concatenate([across, swap(jnp.stack(rest), "x_lo")], 0)
    left, right = [], []
    for even in (near, across):
        left += [even[..., :half], swap(even[..., :half], "z")]
        right += [even[..., half:], by_pair(neighbour(even[..., half:]))]
    return [jnp.concatenate(pieces, 0).reshape(-1, half) for pieces in (left, right)]


def fold_x(partial):
    rows, width = partial.shape
    halves = partial.reshape(2, 2, 4, rows // 16, width)
    other = swap(halves[1], "x_lo")
    return (halves[0].astype(F32) + other.astype(F32)).astype(BF)


def fold_z(folded):
    half = folded.shape[-1] // 2
    even, odd = folded[0], folded[1]
    other = jnp.concatenate([swap(odd[..., :half], "z"), by_pair(neighbour(odd[..., half:]))], 2)
    even = (even.astype(F32) + other.astype(F32)).astype(BF)
    total = even[0].astype(F32)
    for at in range(1, 4):
        total = total + swap(even[at], "z", 2 * at).astype(F32)
    return total


def dot(a, b, dims):
    return lax.dot_general(a, b, (dims, ((), ())), preferred_element_type=F32)


def tangent_kernel(first, index_ref, rows_ref, other_ref, *refs):
    if first:
        pieces, before_ref, outs = refs[:4], refs[4], refs[5:]
        at = 4
    else:
        pieces_ref, before_ref, outs = refs[0], None, refs[1:]
        at = 0
    for k in range(2):
        if first:
            blocks = [pieces[2 * k + i // 2][i % 2] for i in range(4)]
        else:
            blocks = [pieces_ref[i, k] for i in range(4)]
            at = 0
        total = before_ref[k] if first else 0.0
        for block in blocks:
            start = pl.multiple_of(index_ref[at] * 256, 256)
            rows = jnp.concatenate([ref[:, pl.ds(start, 256)] for ref in (rows_ref, other_ref)], 0)
            total = total + dot(block, rows, ((1,), (1,)))
            at += 1
        width = outs[0].shape[2]
        for place, out in enumerate(outs):
            out[k] = total[:, place * width : (place + 1) * width]


def act_kernel(projected_ref, own_ref, other_ref, tangent_ref, act_ref):
    gate, up = [own_ref[k] + other_ref[k] for k in range(2)]
    tangent_ref[0], tangent_ref[1] = gate, up
    silu_value, silu_slope, _ = silu_parts(projected_ref[0])
    act_ref[...] = (silu_slope * gate * projected_ref[1] + silu_value * up).astype(BF)


STEPS = 4


def tangent_call(first, index, rows, pieces, before, out_shape):
    hidden, depth = pieces[0].shape[-2:]
    chunk = hidden // STEPS

    def spec(size):
        return pl.BlockSpec((2, chunk, size), lambda i, index: (0, i, 0))

    if first:
        piece_specs = [spec(depth)] * 4
    else:
        piece_specs = [pl.BlockSpec((4, 2, chunk, depth), lambda i, index: (0, 0, i, 0))]
    return pl.pallas_call(
        lambda *refs: tangent_kernel(first, *refs),
        out_shape=out_shape,
        grid_spec=pltpu.PrefetchScalarGridSpec(
            num_scalar_prefetch=1,
            grid=(STEPS,),
            in_specs=[pl.BlockSpec(r.shape, lambda i, index: (0, 0)) for r in rows]
            + piece_specs
            + [spec(b.shape[2]) for b in before],
            out_specs=[spec(o.shape[2]) for o in out_shape],
        ),
        compiler_params=pltpu.CompilerParams(vmem_limit_bytes=32 * 2**20),
        cost_estimate=pl.CostEstimate(
            flops=8 * hidden * depth * rows[0].shape[0] * 4,
            bytes_accessed=16 * hidden * depth,
            transcendentals=0,
        ),
    )(index, *rows, *pieces, *before)


def curvature_kernel(index_ref, beta_ref, columns_ref, *refs):
    blocks, (current_ref, earlier_ref, shifted_ref, sums_ref) = refs[:4], refs[4:]
    curvature = 0.0
    for at, block in enumerate(blocks):
        rows = jnp.concatenate([columns_ref[index_ref[4 * at + y]] for y in range(4)], 0)
        grads = jnp.concatenate([block[y] for y in range(4)], 1)
        curvature = curvature + dot(grads, rows, ((1,), (0,)))
    current = current_ref[...].astype(F32)
    shifted = curvature - beta_ref[0, 0] * earlier_ref[...].astype(F32)
    shifted_ref[...] = shifted

    def row(product):
        lanes = jnp.sum(product, 0, keepdims=True)
        return lanes[:, :128] + lanes[:, 128:]

    @pl.when(pl.program_id(0) == 0)
    def _():
        sums_ref[...] = jnp.zeros_like(sums_ref)

    parts = [row(p) for p in (curvature * current, shifted * shifted, shifted * current, current * current)]
    sums_ref[...] += jnp.concatenate(parts + [jnp.zeros((4, 128), F32)], 0)


def scale_kernel(entry_count, sums_ref, shifted_ref, current_ref, out_ref, rayleigh_ref, offdiagonal_ref):
    sums = jnp.sum(jnp.sum(sums_ref[...], 0), 1, keepdims=True)
    inner, square, mixed, norm = [sums[k : k + 1] for k in range(4)]
    rayleigh = inner / entry_count
    square = (square - 2.0 * rayleigh * mixed + rayleigh * rayleigh * norm) / entry_count
    offdiagonal = jnp.sqrt(jnp.maximum(square, 0.0) + 1e-06)
    rayleigh_ref[...] = jnp.broadcast_to(rayleigh, rayleigh_ref.shape)
    offdiagonal_ref[...] = jnp.broadcast_to(offdiagonal, offdiagonal_ref.shape)
    residual = shifted_ref[...] - rayleigh * current_ref[...].astype(F32)
    out_ref[...] = (residual / offdiagonal).astype(BF)


def per_device(tokens, targets, gate_up, down_weight, direction, previous, beta_prev):
    width = tokens.shape[1]
    hidden = down_weight.shape[0]
    own_rows = direction.shape[0]
    token_total = tokens.shape[0] * 256
    gate_up_t = gate_up.transpose(1, 2, 0).reshape(2 * hidden, width)
    current_t = direction.transpose(1, 2, 0).reshape(2 * hidden, own_rows)
    earlier_t = previous.transpose(1, 2, 0).reshape(2 * hidden, own_rows)
    x_hi, y_at, core, x_lo, z_at = (lax.axis_index(n) for n in AXES)

    def owner(a, y, c):
        return ((x_hi ^ a) * 4 + y) * 2 + (core ^ c)

    index = jnp.stack([owner(0, y, 0) for y in range(4)] + [owner(1, y_at ^ d, 0) for d in (0, 1, 3, 2, 0, 3, 1, 2)])

    current_far = swap(current_t, "x_hi")
    near = lax.all_gather(current_t, "y")

    even, current_far = lax.optimization_barrier((gather_even(tokens), current_far))
    far = []
    for rows, step in ((current_far[:hidden], 1), (current_far[hidden:], 3)):
        pair = jnp.stack([rows, swap(rows, "y", step)])
        far += [pair, swap(pair, "y", 4 - step)]
    group_rows = gather_x(*gather_z(even)).reshape(-1, width)
    other_rows = swap(group_rows, "core")

    projected = dot(gate_up_t, group_rows, ((1,), (1,)))
    projected, near = lax.optimization_barrier((projected, near))
    gate_pre, up_pre = projected[:hidden], projected[hidden:]
    silu_value, silu_slope, silu_curve = silu_parts(gate_pre)
    hidden_act = (silu_value * up_pre).astype(BF)
    output_part = dot(hidden_act, down_weight, ((0,), (0,))).astype(BF)
    def cut(value, start, size):
        return lax.dynamic_slice_in_dim(value, start * own_rows, size * own_rows, value.ndim - 1)

    both = jnp.stack([cut(group_rows, x_hi * 8, 8), swap(cut(group_rows, 8 - x_hi * 8, 8), "x_hi")])

    near, both, *far = lax.optimization_barrier((near, both, *far))
    output_fold = fold_x(output_part)

    def halves(value):
        return value.reshape(2, hidden, value.shape[1])

    chunk = hidden // STEPS
    count = group_rows.shape[0]

    def sum_of(size):
        return jax.ShapeDtypeStruct((2, hidden, size), F32)

    own_shape = sum_of(count)
    rows_pair = (group_rows, other_rows)
    near_sums = tangent_call(0, index, rows_pair, [near.reshape(4, 2, hidden, -1)], [], [sum_of(2 * count)])
    own_sums, other_sums = tangent_call(
        1, index, rows_pair, far, near_sums, [own_shape, own_shape]
    )
    own_sums, output_fold = lax.optimization_barrier((own_sums, output_fold))
    step_spec = pl.BlockSpec((2, chunk, count), lambda i: (0, i, 0))
    tangent, tangent_act = pl.pallas_call(
        act_kernel,
        out_shape=(own_shape, jax.ShapeDtypeStruct((hidden, count), BF)),
        grid=(STEPS,),
        in_specs=[step_spec] * 3,
        out_specs=(step_spec, pl.BlockSpec((chunk, count), lambda i: (i, 0))),
        compiler_params=pltpu.CompilerParams(vmem_limit_bytes=32 * 2**20),
        cost_estimate=pl.CostEstimate(flops=2**20, bytes_accessed=2 * 2**20, transcendentals=2**16),
    )(halves(projected), own_sums, swap(other_sums, "core"))
    tangent_gate, tangent_up = tangent[0], tangent[1]
    tangent_part = dot(tangent_act, down_weight, ((0,), (0,))).astype(BF)
    tangent_fold = fold_x(tangent_part)


    sums = fold_z(jnp.concatenate([output_fold, tangent_fold], 2))
    output_sum, tangent_sum = sums[: targets.shape[0]], sums[targets.shape[0] :]
    error_rows = ((output_sum - targets.astype(F32)) / token_total).astype(BF)
    tangent_error = (tangent_sum / token_total).astype(BF)
    errors = jnp.concatenate([error_rows, tangent_error], 1)
    errors, both = lax.optimization_barrier((errors, both))
    own_columns = jnp.stack(
        [cut(both, y_at * 2, 2)] + [swap(cut(both, (y_at ^ d) * 2, 2), "y", d) for d in range(1, 4)], 1
    )
    own_columns = jnp.stack(
        [cut(own_columns, core, 1), swap(cut(own_columns, 1 - core, 1), "core")], 1
    ).reshape(16, count, own_rows)
    error_rows, tangent_error = gather_both(errors)
    back_error = dot(down_weight, error_rows, ((1,), (1,)))
    back_tangent = dot(down_weight, tangent_error, ((1,), (1,)))

    grad_gate = back_tangent * up_pre * silu_slope + back_error * (
        tangent_up * silu_slope + up_pre * silu_curve * tangent_gate
    )
    grad_up = back_tangent * silu_value + back_error * silu_slope * tangent_gate
    tangent_grad = jnp.concatenate([grad_gate, grad_up], 0).astype(BF)
    tangent_grad, own_columns = lax.optimization_barrier((tangent_grad, own_columns))
    grad_far = swap(tangent_grad, "x_hi")
    blocks = []
    for piece in (tangent_grad, grad_far):
        piece = lax.all_gather(piece, "y")
        blocks += [piece, swap(piece, "core")]
    groups = jnp.stack([(a * 2 + c) * 4 + (y_at ^ y) for a in range(2) for c in range(2) for y in range(4)])
    rows = 2 * hidden // STEPS
    row_spec = pl.BlockSpec((rows, own_rows), lambda i, index: (i, 0))
    shifted, sums = pl.pallas_call(
        curvature_kernel,
        out_shape=(
            jax.ShapeDtypeStruct((2 * hidden, own_rows), F32),
            jax.ShapeDtypeStruct((8, 128), F32),
        ),
        grid_spec=pltpu.PrefetchScalarGridSpec(
            num_scalar_prefetch=1,
            grid=(STEPS,),
            in_specs=[
                pl.BlockSpec(memory_space=pltpu.SMEM),
                pl.BlockSpec(own_columns.shape, lambda i, index: (0, 0, 0)),
            ]
            + [pl.BlockSpec((4, rows, count), lambda i, index: (0, i, 0))] * 4
            + [row_spec] * 2,
            out_specs=(row_spec, pl.BlockSpec((8, 128), lambda i, index: (0, 0))),
        ),
        compiler_params=pltpu.CompilerParams(vmem_limit_bytes=32 * 2**20),
        cost_estimate=pl.CostEstimate(flops=2**30, bytes_accessed=7 * 2**20, transcendentals=0),
    )(groups, beta_prev.reshape(1, 1), own_columns, *blocks, current_t, earlier_t)

    for axes in (("z",), AXES[:4]):
        size = lax.axis_size(axes)
        if axes != ("z",):
            sums = sums.sum(0)
        sums = lax.all_to_all(jnp.broadcast_to(sums[None], (size, 8, 128)), axes, 0, 0, tiled=True)

    row_spec = pl.BlockSpec((rows, own_rows), lambda i: (i, 0))
    one_spec = pl.BlockSpec((1, 128), lambda i: (0, 0))
    new_direction, rayleigh, offdiagonal = pl.pallas_call(
        lambda *refs: scale_kernel(2 * own_rows * hidden * 256, *refs),
        out_shape=(
            jax.ShapeDtypeStruct((2 * hidden, own_rows), BF),
            jax.ShapeDtypeStruct((1, 128), F32),
            jax.ShapeDtypeStruct((1, 128), F32),
        ),
        grid=(STEPS,),
        in_specs=[pl.BlockSpec(sums.shape, lambda i: (0, 0, 0)), row_spec, row_spec],
        out_specs=(row_spec, one_spec, one_spec),
        compiler_params=pltpu.CompilerParams(vmem_limit_bytes=32 * 2**20),
        cost_estimate=pl.CostEstimate(flops=2**20, bytes_accessed=2 * 2**20, transcendentals=0),
    )(sums, shifted, current_t)
    rayleigh, offdiagonal = rayleigh[0, 0], offdiagonal[0, 0]
    new_direction = new_direction.reshape(2, hidden, own_rows).transpose(2, 0, 1)
    return (new_direction, rayleigh, offdiagonal)


def solution(mesh):
    fine = Mesh(mesh.devices.reshape(SIZES), AXES)
    fsdp, tensor = AXES[:3], AXES[3:]
    placed = (
        P(fsdp + tensor, None),
        P(fsdp + tensor, None),
        P(None, None, tensor),
        P(tensor, None),
        P(fsdp, None, tensor),
        P(fsdp, None, tensor),
        P(),
    )
    return jax.shard_map(
        per_device,
        mesh=fine,
        in_specs=placed,
        out_specs=(P(fsdp, None, tensor), P(), P()),
        check_vma=False,
    )
```

```python
import jax
import jax.numpy as jnp
from jax import lax
from jax.experimental import pallas as pl
from jax.experimental.pallas import tpu as pltpu
from jax.sharding import Mesh, PartitionSpec as P

BF = jnp.bfloat16
F32 = jnp.float32
AXES = ("x_hi", "y", "core", "x_lo", "z")
SIZES = (2, 4, 2, 2, 8)


def swap(value, axis, step=1):
    size = lax.axis_size(axis)
    return lax.ppermute(value, axis, [(i, i ^ step) for i in range(size)])


def silu_parts(gate_pre):
    sigma_gate = jax.nn.sigmoid(gate_pre)
    silu_value = gate_pre * sigma_gate
    silu_slope = sigma_gate * (1.0 + gate_pre * (1.0 - sigma_gate))
    silu_curve = sigma_gate * (1.0 - sigma_gate) * (2.0 + gate_pre * (1.0 - 2.0 * sigma_gate))
    return (silu_value, silu_slope, silu_curve)


def neighbour(value):
    return lax.ppermute(value, "z", [(i, (i + 1) % 8 if i % 2 else (i - 1) % 8) for i in range(8)])


def by_pair(value):
    at = lax.axis_index("z") % 4
    pairs = value.reshape(2, 2, *value.shape[1:])
    turned = jnp.where((at == 1) | (at == 2), lax.rev(pairs, (1,)), lax.rev(pairs, (0, 1)))
    return turned.reshape(value.shape)


def gather_even(block):
    return jnp.stack([block] + [swap(block, "z", d) for d in (2, 4, 6)])


def gather_z(even):
    half = even.shape[2] // 2
    odd = jnp.concatenate([swap(even[..., :half], "z"), by_pair(neighbour(even[..., half:]))], 2)
    return even, odd


def gather_x(even, odd):
    return jnp.concatenate([even, odd, swap(even, "x_lo"), swap(odd, "x_lo")], 0)


def gather_both(block):
    half = block.shape[1] // 2
    rest = [swap(block, "z", d) for d in (2, 4, 6)]
    across = swap(block, "x_lo")[None]
    near = jnp.stack([block] + rest)
    across = jnp.concatenate([across, swap(jnp.stack(rest), "x_lo")], 0)
    left, right = [], []
    for even in (near, across):
        left += [even[..., :half], swap(even[..., :half], "z")]
        right += [even[..., half:], by_pair(neighbour(even[..., half:]))]
    return [jnp.concatenate(pieces, 0).reshape(-1, half) for pieces in (left, right)]


def fold_x(partial):
    rows, width = partial.shape
    halves = partial.reshape(2, 2, 4, rows // 16, width)
    other = swap(halves[1], "x_lo")
    return (halves[0].astype(F32) + other.astype(F32)).astype(BF)


def fold_z(folded):
    half = folded.shape[-1] // 2
    even, odd = folded[0], folded[1]
    other = jnp.concatenate([swap(odd[..., :half], "z"), by_pair(neighbour(odd[..., half:]))], 2)
    even = (even.astype(F32) + other.astype(F32)).astype(BF)
    total = even[0].astype(F32)
    for at in range(1, 4):
        total = total + swap(even[at], "z", 2 * at).astype(F32)
    return total


def dot(a, b, dims):
    return lax.dot_general(a, b, (dims, ((), ())), preferred_element_type=F32)


def tangent_kernel(first, index_ref, rows_ref, other_ref, *refs):
    if first:
        pieces, before_ref, outs = refs[:4], refs[4], refs[5:]
        at = 4
    else:
        pieces_ref, before_ref, outs = refs[0], None, refs[1:]
        at = 0
    for k in range(2):
        if first:
            blocks = [pieces[2 * k + i // 2][i % 2] for i in range(4)]
        else:
            blocks = [pieces_ref[i, k] for i in range(4)]
            at = 0
        total = before_ref[k] if first else 0.0
        for block in blocks:
            start = pl.multiple_of(index_ref[at] * 256, 256)
            rows = jnp.concatenate([ref[:, pl.ds(start, 256)] for ref in (rows_ref, other_ref)], 0)
            total = total + dot(block, rows, ((1,), (1,)))
            at += 1
        width = outs[0].shape[2]
        for place, out in enumerate(outs):
            out[k] = total[:, place * width : (place + 1) * width]


def act_kernel(projected_ref, own_ref, other_ref, tangent_ref, act_ref):
    gate, up = [own_ref[k] + other_ref[k] for k in range(2)]
    tangent_ref[0], tangent_ref[1] = gate, up
    silu_value, silu_slope, _ = silu_parts(projected_ref[0])
    act_ref[...] = (silu_slope * gate * projected_ref[1] + silu_value * up).astype(BF)


STEPS = 4


def tangent_call(first, index, rows, pieces, before, out_shape):
    hidden, depth = pieces[0].shape[-2:]
    chunk = hidden // STEPS

    def spec(size):
        return pl.BlockSpec((2, chunk, size), lambda i, index: (0, i, 0))

    if first:
        piece_specs = [spec(depth)] * 4
    else:
        piece_specs = [pl.BlockSpec((4, 2, chunk, depth), lambda i, index: (0, 0, i, 0))]
    return pl.pallas_call(
        lambda *refs: tangent_kernel(first, *refs),
        out_shape=out_shape,
        grid_spec=pltpu.PrefetchScalarGridSpec(
            num_scalar_prefetch=1,
            grid=(STEPS,),
            in_specs=[pl.BlockSpec(r.shape, lambda i, index: (0, 0)) for r in rows]
            + piece_specs
            + [spec(b.shape[2]) for b in before],
            out_specs=[spec(o.shape[2]) for o in out_shape],
        ),
        compiler_params=pltpu.CompilerParams(vmem_limit_bytes=32 * 2**20),
        cost_estimate=pl.CostEstimate(
            flops=8 * hidden * depth * rows[0].shape[0] * 4,
            bytes_accessed=16 * hidden * depth,
            transcendentals=0,
        ),
    )(index, *rows, *pieces, *before)


def curvature_kernel(index_ref, beta_ref, columns_ref, *refs):
    blocks, (current_ref, earlier_ref, shifted_ref, sums_ref) = refs[:4], refs[4:]
    curvature = 0.0
    for at, block in enumerate(blocks):
        rows = jnp.concatenate([columns_ref[index_ref[4 * at + y]] for y in range(4)], 0)
        grads = jnp.concatenate([block[y] for y in range(4)], 1)
        curvature = curvature + dot(grads, rows, ((1,), (0,)))
    current = current_ref[...].astype(F32)
    shifted = curvature - beta_ref[0, 0] * earlier_ref[...].astype(F32)
    shifted_ref[...] = shifted

    def row(product):
        lanes = jnp.sum(product, 0, keepdims=True)
        return lanes[:, :128] + lanes[:, 128:]

    @pl.when(pl.program_id(0) == 0)
    def _():
        sums_ref[...] = jnp.zeros_like(sums_ref)

    parts = [row(p) for p in (curvature * current, shifted * shifted, shifted * current, current * current)]
    sums_ref[...] += jnp.concatenate(parts + [jnp.zeros((4, 128), F32)], 0)


def scale_kernel(entry_count, sums_ref, shifted_ref, current_ref, out_ref, rayleigh_ref, offdiagonal_ref):
    sums = jnp.sum(jnp.sum(sums_ref[...], 0), 1, keepdims=True)
    inner, square, mixed, norm = [sums[k : k + 1] for k in range(4)]
    rayleigh = inner / entry_count
    square = (square - 2.0 * rayleigh * mixed + rayleigh * rayleigh * norm) / entry_count
    offdiagonal = jnp.sqrt(jnp.maximum(square, 0.0) + 1e-06)
    rayleigh_ref[...] = jnp.broadcast_to(rayleigh, rayleigh_ref.shape)
    offdiagonal_ref[...] = jnp.broadcast_to(offdiagonal, offdiagonal_ref.shape)
    residual = shifted_ref[...] - rayleigh * current_ref[...].astype(F32)
    out_ref[...] = (residual / offdiagonal).astype(BF)


def per_device(tokens, targets, gate_up, down_weight, direction, previous, beta_prev):
    width = tokens.shape[1]
    hidden = down_weight.shape[0]
    own_rows = direction.shape[0]
    token_total = tokens.shape[0] * 256
    gate_up_t = gate_up.transpose(1, 2, 0).reshape(2 * hidden, width)
    current_t = direction.transpose(1, 2, 0).reshape(2 * hidden, own_rows)
    earlier_t = previous.transpose(1, 2, 0).reshape(2 * hidden, own_rows)
    x_hi, y_at, core, x_lo, z_at = (lax.axis_index(n) for n in AXES)

    def owner(a, y, c):
        return ((x_hi ^ a) * 4 + y) * 2 + (core ^ c)

    index = jnp.stack([owner(0, y, 0) for y in range(4)] + [owner(1, y_at ^ d, 0) for d in (0, 1, 3, 2, 0, 3, 1, 2)])

    current_far = swap(current_t, "x_hi")
    near = lax.all_gather(current_t, "y")

    even, odd = gather_z(gather_even(tokens))
    odd, current_far = lax.optimization_barrier((odd, current_far))
    far = []
    for rows, step in ((current_far[:hidden], 1), (current_far[hidden:], 3)):
        pair = jnp.stack([rows, swap(rows, "y", step)])
        far += [pair, swap(pair, "y", 4 - step)]
    group_rows = gather_x(even, odd).reshape(-1, width)
    other_rows = swap(group_rows, "core")

    projected = dot(gate_up_t, group_rows, ((1,), (1,)))
    projected, near = lax.optimization_barrier((projected, near))
    gate_pre, up_pre = projected[:hidden], projected[hidden:]
    silu_value, silu_slope, silu_curve = silu_parts(gate_pre)
    hidden_act = (silu_value * up_pre).astype(BF)
    output_part = dot(hidden_act, down_weight, ((0,), (0,))).astype(BF)
    def cut(value, start, size):
        return lax.dynamic_slice_in_dim(value, start * own_rows, size * own_rows, value.ndim - 1)

    both = jnp.stack([cut(group_rows, x_hi * 8, 8), swap(cut(group_rows, 8 - x_hi * 8, 8), "x_hi")])

    near, both, *far = lax.optimization_barrier((near, both, *far))
    output_fold = fold_x(output_part)

    def halves(value):
        return value.reshape(2, hidden, value.shape[1])

    chunk = hidden // STEPS
    count = group_rows.shape[0]

    def sum_of(size):
        return jax.ShapeDtypeStruct((2, hidden, size), F32)

    own_shape = sum_of(count)
    rows_pair = (group_rows, other_rows)
    near_sums = tangent_call(0, index, rows_pair, [near.reshape(4, 2, hidden, -1)], [], [sum_of(2 * count)])
    own_sums, other_sums = tangent_call(
        1, index, rows_pair, far, near_sums, [own_shape, own_shape]
    )
    own_sums, output_fold = lax.optimization_barrier((own_sums, output_fold))
    step_spec = pl.BlockSpec((2, chunk, count), lambda i: (0, i, 0))
    tangent, tangent_act = pl.pallas_call(
        act_kernel,
        out_shape=(own_shape, jax.ShapeDtypeStruct((hidden, count), BF)),
        grid=(STEPS,),
        in_specs=[step_spec] * 3,
        out_specs=(step_spec, pl.BlockSpec((chunk, count), lambda i: (i, 0))),
        compiler_params=pltpu.CompilerParams(vmem_limit_bytes=32 * 2**20),
        cost_estimate=pl.CostEstimate(flops=2**20, bytes_accessed=2 * 2**20, transcendentals=2**16),
    )(halves(projected), own_sums, swap(other_sums, "core"))
    tangent_gate, tangent_up = tangent[0], tangent[1]
    tangent_part = dot(tangent_act, down_weight, ((0,), (0,))).astype(BF)
    tangent_fold = fold_x(tangent_part)


    sums = fold_z(jnp.concatenate([output_fold, tangent_fold], 2))
    output_sum, tangent_sum = sums[: targets.shape[0]], sums[targets.shape[0] :]
    error_rows = ((output_sum - targets.astype(F32)) / token_total).astype(BF)
    tangent_error = (tangent_sum / token_total).astype(BF)
    errors = jnp.concatenate([error_rows, tangent_error], 1)
    errors, both = lax.optimization_barrier((errors, both))
    own_columns = jnp.stack(
        [cut(both, y_at * 2, 2)] + [swap(cut(both, (y_at ^ d) * 2, 2), "y", d) for d in range(1, 4)], 1
    )
    own_columns = jnp.stack(
        [cut(own_columns, core, 1), swap(cut(own_columns, 1 - core, 1), "core")], 1
    ).reshape(16, count, own_rows)
    error_rows, tangent_error = gather_both(errors)
    back_error = dot(down_weight, error_rows, ((1,), (1,)))
    back_tangent = dot(down_weight, tangent_error, ((1,), (1,)))

    grad_gate = back_tangent * up_pre * silu_slope + back_error * (
        tangent_up * silu_slope + up_pre * silu_curve * tangent_gate
    )
    grad_up = back_tangent * silu_value + back_error * silu_slope * tangent_gate
    tangent_grad = jnp.concatenate([grad_gate, grad_up], 0).astype(BF)
    tangent_grad, own_columns = lax.optimization_barrier((tangent_grad, own_columns))
    grad_far = swap(tangent_grad, "x_hi")
    blocks = []
    for piece in (tangent_grad, grad_far):
        piece = lax.all_gather(piece, "y")
        blocks += [piece, swap(piece, "core")]
    groups = jnp.stack([(a * 2 + c) * 4 + (y_at ^ y) for a in range(2) for c in range(2) for y in range(4)])
    rows = 2 * hidden // STEPS
    row_spec = pl.BlockSpec((rows, own_rows), lambda i, index: (i, 0))
    shifted, sums = pl.pallas_call(
        curvature_kernel,
        out_shape=(
            jax.ShapeDtypeStruct((2 * hidden, own_rows), F32),
            jax.ShapeDtypeStruct((8, 128), F32),
        ),
        grid_spec=pltpu.PrefetchScalarGridSpec(
            num_scalar_prefetch=1,
            grid=(STEPS,),
            in_specs=[
                pl.BlockSpec(memory_space=pltpu.SMEM),
                pl.BlockSpec(own_columns.shape, lambda i, index: (0, 0, 0)),
            ]
            + [pl.BlockSpec((4, rows, count), lambda i, index: (0, i, 0))] * 4
            + [row_spec] * 2,
            out_specs=(row_spec, pl.BlockSpec((8, 128), lambda i, index: (0, 0))),
        ),
        compiler_params=pltpu.CompilerParams(vmem_limit_bytes=32 * 2**20),
        cost_estimate=pl.CostEstimate(flops=2**30, bytes_accessed=7 * 2**20, transcendentals=0),
    )(groups, beta_prev.reshape(1, 1), own_columns, *blocks, current_t, earlier_t)

    for axes in (("z",), AXES[:4]):
        size = lax.axis_size(axes)
        if axes != ("z",):
            sums = sums.sum(0)
        sums = lax.all_to_all(jnp.broadcast_to(sums[None], (size, 8, 128)), axes, 0, 0, tiled=True)

    row_spec = pl.BlockSpec((rows, own_rows), lambda i: (i, 0))
    one_spec = pl.BlockSpec((1, 128), lambda i: (0, 0))
    new_direction, rayleigh, offdiagonal = pl.pallas_call(
        lambda *refs: scale_kernel(2 * own_rows * hidden * 256, *refs),
        out_shape=(
            jax.ShapeDtypeStruct((2 * hidden, own_rows), BF),
            jax.ShapeDtypeStruct((1, 128), F32),
            jax.ShapeDtypeStruct((1, 128), F32),
        ),
        grid=(STEPS,),
        in_specs=[pl.BlockSpec(sums.shape, lambda i: (0, 0, 0)), row_spec, row_spec],
        out_specs=(row_spec, one_spec, one_spec),
        compiler_params=pltpu.CompilerParams(vmem_limit_bytes=32 * 2**20),
        cost_estimate=pl.CostEstimate(flops=2**20, bytes_accessed=2 * 2**20, transcendentals=0),
    )(sums, shifted, current_t)
    rayleigh, offdiagonal = rayleigh[0, 0], offdiagonal[0, 0]
    new_direction = new_direction.reshape(2, hidden, own_rows).transpose(2, 0, 1)
    return (new_direction, rayleigh, offdiagonal)


def solution(mesh):
    fine = Mesh(mesh.devices.reshape(SIZES), AXES)
    fsdp, tensor = AXES[:3], AXES[3:]
    placed = (
        P(fsdp + tensor, None),
        P(fsdp + tensor, None),
        P(None, None, tensor),
        P(tensor, None),
        P(fsdp, None, tensor),
        P(fsdp, None, tensor),
        P(),
    )
    return jax.shard_map(
        per_device,
        mesh=fine,
        in_specs=placed,
        out_specs=(P(fsdp, None, tensor), P(), P()),
        check_vma=False,
    )
```
